256 devices in a mesh: gx: 16 (over z_lo, x), gy: 16 (over y, z_hi, core).
Axes of the slice: x: 4, y: 4, z: 8 (z_hi: 2, z_lo: 4; z = z_hi * 4 + z_lo), core: 2. Of those that a mesh axis runs over, the one named last changes fastest.
Arguments:
- field: bfloat16 [64, 128, 1024], P('gx', 'gy'), may hold values from -6 to 6
- cotangent: bfloat16 [64, 128, 1024], P('gx', 'gy'), may hold values from -6 to 6
- kernel_one: bfloat16 [27, 32, 32], replicated, may hold values from -0.21875 to 0.21875
- kernel_two: bfloat16 [27, 32, 32], replicated, may hold values from -0.21875 to 0.21875
- spectral_weight: float32 [2, 4608, 32, 32], P(None, ('gx', 'gy')), may hold values from -9 to 9
Outputs:
- field_grad: bfloat16 [64, 128, 1024], P('gx', 'gy')
- kernel_one_grad: float32 [27, 32, 32], replicated
- kernel_two_grad: float32 [27, 32, 32], replicated
- spectral_grad: float32 [2, 4608, 32, 32], P(None, ('gx', 'gy'))
The draws below stay inside these ranges and needn't reach their ends.
All inputs are finite; a program needn't handle non-finite values.
Results may differ from the reference program's by a relative error of at most 0.0055.
Values may be sent and summed in bfloat16 or wider, within the bound.
A program may use at most 128 MiB of HBM per device.

```python
import math
import jax
import jax.numpy as jnp
from jax import lax

C = 32
MX = 24
MY = 24
MZ = 8
NZ = 32
NX = 64
NY = 128
MODES = 4608


def level_of(key, extent, cuts, low, high):
    level = 1.0
    for axis_at, blocks in cuts:
        heights = jax.random.uniform(jax.random.fold_in(jax.random.fold_in(key, 6), axis_at), (blocks,), jnp.float32, low / len(cuts), high / len(cuts))
        level = level * jnp.repeat(jnp.exp(heights), extent[axis_at] // blocks).reshape((-1,) + (1,) * (len(extent) - 1 - axis_at))
    return level


def noise(rng, extent, scale, most, split=(), kind=jnp.bfloat16):
    factor_of = level_of(rng, extent, split, -0.22, 0.18) if split else 1.0
    drawn = jax.random.normal(rng, extent, jnp.float32) * scale * factor_of
    return jnp.minimum(jnp.maximum(drawn, -most), most).astype(kind)


def setup_inputs(seed: int = 0) -> dict:
    keys = jax.random.split(jax.random.key(seed), 6)
    return {
        "field": noise(keys[0], (NX, NY, NZ * C), 1.0, 6.0, ((0, 16), (1, 16))),
        "cotangent": noise(keys[1], (NX, NY, NZ * C), 1.0, 6.0, ((0, 16), (1, 16))),
        "kernel_one": noise(keys[2], (27, C, C), (27 * C) ** -0.5, 0.21875),
        "kernel_two": noise(keys[3], (27, C, C), (27 * C) ** -0.5, 0.21875),
        "spectral_weight": noise(keys[4], (2, MODES, C, C), 1.5, 9.0, ((1, 256),), jnp.float32),
    }


HIGH = lax.Precision.HIGHEST

def phase(coords, freqs, length):
    turns = coords[:, None] * freqs[None, :] % length
    angle = turns.astype(jnp.float32) * (2.0 * math.pi / length)
    return (jnp.cos(angle), jnp.sin(angle))

def kept(length, count):
    half = count // 2
    return jnp.concatenate([jnp.arange(half, dtype=jnp.int32), length - half + jnp.arange(half, dtype=jnp.int32)]).astype(jnp.int32)

def tables(xs, ys, nx, ny):
    cos_x, sin_x = phase(xs, kept(nx, MX), nx)
    cos_y, sin_y = phase(ys, kept(ny, MY), ny)
    cos_z, sin_z = phase(jnp.arange(NZ, dtype=jnp.int32), jnp.arange(MZ, dtype=jnp.int32), NZ)
    return (cos_x, sin_x, cos_y, sin_y, cos_z, sin_z)

def analyse(field32, tabs):
    cos_x, sin_x, cos_y, sin_y, cos_z, sin_z = tabs
    zre = jnp.einsum('xyzc,zk->xykc', field32, cos_z, precision=HIGH)
    zim = -jnp.einsum('xyzc,zk->xykc', field32, sin_z, precision=HIGH)
    yre = jnp.einsum('xykc,yj->xjkc', zre, cos_y, precision=HIGH) + jnp.einsum('xykc,yj->xjkc', zim, sin_y, precision=HIGH)
    yim = jnp.einsum('xykc,yj->xjkc', zim, cos_y, precision=HIGH) - jnp.einsum('xykc,yj->xjkc', zre, sin_y, precision=HIGH)
    are = jnp.einsum('xjkc,xi->ikjc', yre, cos_x, precision=HIGH) + jnp.einsum('xjkc,xi->ikjc', yim, sin_x, precision=HIGH)
    aim = jnp.einsum('xjkc,xi->ikjc', yim, cos_x, precision=HIGH) - jnp.einsum('xjkc,xi->ikjc', yre, sin_x, precision=HIGH)
    return (are.reshape(-1, field32.shape[3]), aim.reshape(-1, field32.shape[3]))

def synthesise(real_part, imag_part, tabs):
    cos_x, sin_x, cos_y, sin_y, cos_z, sin_z = tabs
    are = real_part.reshape(MX, MZ, MY, -1)
    aim = imag_part.reshape(MX, MZ, MY, -1)
    bre = jnp.einsum('ikjc,xi->xjkc', are, cos_x, precision=HIGH) - jnp.einsum('ikjc,xi->xjkc', aim, sin_x, precision=HIGH)
    bim = jnp.einsum('ikjc,xi->xjkc', aim, cos_x, precision=HIGH) + jnp.einsum('ikjc,xi->xjkc', are, sin_x, precision=HIGH)
    cre = jnp.einsum('xjkc,yj->xykc', bre, cos_y, precision=HIGH) - jnp.einsum('xjkc,yj->xykc', bim, sin_y, precision=HIGH)
    cim = jnp.einsum('xjkc,yj->xykc', bim, cos_y, precision=HIGH) + jnp.einsum('xjkc,yj->xykc', bre, sin_y, precision=HIGH)
    return jnp.einsum('xykc,zk->xyzc', cre, cos_z, precision=HIGH) - jnp.einsum('xykc,zk->xyzc', cim, sin_z, precision=HIGH)

def mode_scale(modes, ncells):
    kz = modes // MY % MZ
    return (jnp.where(kz == 0, 1.0, 2.0) / ncells).astype(jnp.float32)[:, None]

def pad_all(values):
    return jnp.pad(values, ((1, 1), (1, 1), (1, 1), (0, 0)))

def conv_sum(padded, kernel, len_x, len_y):
    total = jnp.zeros((len_x * len_y * NZ, kernel.shape[2]), jnp.float32)
    for offset in range(27):
        a, b, e = (offset // 9, offset // 3 % 3, offset % 3)
        piece = padded[a:a + len_x, b:b + len_y, e:e + NZ].reshape(-1, kernel.shape[1])
        total = total + jnp.dot(piece, kernel[offset], preferred_element_type=jnp.float32)
    return total.reshape(len_x, len_y, NZ, kernel.shape[2])

def conv_back(padded, kernel, len_x, len_y):
    total = jnp.zeros((len_x * len_y * NZ, kernel.shape[1]), jnp.float32)
    for offset in range(27):
        a, b, e = (offset // 9, offset // 3 % 3, offset % 3)
        piece = padded[2 - a:2 - a + len_x, 2 - b:2 - b + len_y, 2 - e:2 - e + NZ].reshape(-1, kernel.shape[2])
        total = total + jnp.dot(piece, kernel[offset].T, preferred_element_type=jnp.float32)
    return total.reshape(len_x, len_y, NZ, kernel.shape[1])

def correlate(padded, grad, len_x, len_y):
    flat_grad = grad.reshape(-1, grad.shape[3])
    terms = []
    for offset in range(27):
        a, b, e = (offset // 9, offset // 3 % 3, offset % 3)
        piece = padded[a:a + len_x, b:b + len_y, e:e + NZ].reshape(-1, padded.shape[3])
        terms.append(jnp.dot(piece.T, flat_grad, preferred_element_type=jnp.float32))
    return jnp.stack(terms)

def mix_modes(xre, xim, wre, wim):
    yre = jnp.einsum('mi,mio->mo', xre, wre, precision=HIGH) - jnp.einsum('mi,mio->mo', xim, wim, precision=HIGH)
    yim = jnp.einsum('mi,mio->mo', xre, wim, precision=HIGH) + jnp.einsum('mi,mio->mo', xim, wre, precision=HIGH)
    return (yre, yim)

def weight_grads(xre, xim, dyre, dyim, wre, wim):
    gre = jnp.einsum('mi,mo->mio', xre, dyre, precision=HIGH) + jnp.einsum('mi,mo->mio', xim, dyim, precision=HIGH)
    gim = jnp.einsum('mi,mo->mio', xre, dyim, precision=HIGH) - jnp.einsum('mi,mo->mio', xim, dyre, precision=HIGH)
    dxre = jnp.einsum('mio,mo->mi', wre, dyre, precision=HIGH) + jnp.einsum('mio,mo->mi', wim, dyim, precision=HIGH)
    dxim = jnp.einsum('mio,mo->mi', wre, dyim, precision=HIGH) - jnp.einsum('mio,mo->mi', wim, dyre, precision=HIGH)
    return (jnp.stack([gre, gim]), dxre, dxim)

def reference(field, cotangent, kernel_one, kernel_two, spectral_weight):
    inputs = field.reshape(NX, NY, NZ, C)
    padded_x = pad_all(inputs)
    pre = conv_sum(padded_x, kernel_one, NX, NY)
    hidden = jax.nn.gelu(pre).astype(jnp.bfloat16)
    padded_h = pad_all(hidden)
    branch = conv_sum(padded_h, kernel_two, NX, NY)
    tabs = tables(jnp.arange(NX, dtype=jnp.int32), jnp.arange(NY, dtype=jnp.int32), NX, NY)
    scale = mode_scale(jnp.arange(MODES, dtype=jnp.int32), NX * NY * NZ)
    xre, xim = analyse(inputs.astype(jnp.float32), tabs)
    yre, yim = mix_modes(xre, xim, spectral_weight[0], spectral_weight[1])
    total = synthesise(yre * scale, yim * scale, tabs) + branch
    _, pull = jax.vjp(jax.nn.gelu, total)
    dtotal = pull(cotangent.reshape(NX, NY, NZ, C).astype(jnp.float32))[0].astype(jnp.bfloat16)
    dhidden = conv_back(pad_all(dtotal), kernel_two, NX, NY)
    _, pull_pre = jax.vjp(jax.nn.gelu, pre)
    dpre = pull_pre(dhidden)[0].astype(jnp.bfloat16)
    kernel_two_grad = correlate(padded_h, dtotal, NX, NY)
    kernel_one_grad = correlate(padded_x, dpre, NX, NY)
    dconv = conv_back(pad_all(dpre), kernel_one, NX, NY)
    dre, dim_part = analyse(dtotal.astype(jnp.float32), tabs)
    spectral_grad, dxre, dxim = weight_grads(xre, xim, dre * scale, dim_part * scale, spectral_weight[0], spectral_weight[1])
    field_grad = (dconv + synthesise(dxre, dxim, tabs)).astype(jnp.bfloat16).reshape(NX, NY, NZ * C)
    return (field_grad, kernel_one_grad, kernel_two_grad, spectral_grad)
```

```python
import math

import jax
import jax.numpy as jnp
import numpy as np
from jax import lax
from jax.experimental import pallas as pl
from jax.experimental.pallas import tpu as pltpu
from jax.sharding import PartitionSpec as P

C = 32
MX = 24
MY = 24
MZ = 8
NZ = 32
NX = 64
NY = 128
PEERS = 16
LX = 4
LY = 8
MESH = pl.DeviceIdType.MESH
F32 = jnp.float32
BF16 = jnp.bfloat16
HIGH = lax.Precision.HIGHEST


def kept(length, count):
    half = count // 2
    return np.concatenate([np.arange(half), length - half + np.arange(half)])


def angles(coords, freqs, length):
    return (coords[:, None] * freqs[None, :] % length) * (2.0 * math.pi / length)


def split(table):
    high = table.astype(BF16)
    low = (table - high.astype(np.float64)).astype(BF16)
    return np.stack([high, low])


def constants():
    az = angles(np.arange(NZ), np.arange(MZ), NZ).reshape(NZ, 2, 4)
    fz = np.stack([np.cos(az), -np.sin(az)], axis=2)
    mz = np.einsum("zhrk,ij->zihrkj", fz, np.eye(C)).reshape(NZ * C, 2 * MZ * C)
    ax = angles(np.arange(NX), kept(NX, MX), NX)
    tx = np.stack([np.cos(ax), np.sin(ax)], axis=-1).reshape(PEERS, LX, MX, 2)
    tx = tx.transpose(0, 2, 1, 3).reshape(PEERS, MX * LX * 2)
    ay = angles(np.arange(NY), kept(NY, MY), NY).reshape(PEERS, LY, 4, 6)
    cy = np.zeros((PEERS, 4, 8, LY))
    sy = np.zeros((PEERS, 4, 8, LY))
    cy[:, :, :6] = np.cos(ay).transpose(0, 2, 3, 1)
    sy[:, :, :6] = np.sin(ay).transpose(0, 2, 3, 1)
    cy = cy.reshape(PEERS, 32, LY)
    sy = sy.reshape(PEERS, 32, LY)
    ty = np.concatenate([cy, sy], axis=2)
    tys = ty.transpose(0, 2, 1)
    return (
        split(mz),
        split(mz.T),
        tx.astype(np.float32),
        ty.astype(np.float32),
        tys.astype(np.float32),
    )


def gelu_parts(x):
    k = math.sqrt(2.0 / math.pi)
    t = jnp.tanh(k * (x + 0.044715 * (x * x * x)))
    cdf = 0.5 * (1.0 + t)
    slope = cdf + x * (0.5 * (1.0 - t * t)) * (k * (1.0 + (3.0 * 0.044715) * (x * x)))
    return x * cdf, slope


def dot(a, b, precision=None):
    return jnp.dot(a, b, preferred_element_type=F32, precision=precision)


def body(
    field, cot, kk, sw, mz, mzs, tx, ty, tys,
    out_field, out_kg, out_sg,
    xe, de, xw, hw, dw, pw, pre, brn, band, cg, zt, sp, dts, dtl,
    s1, r1, s2, r2, xt, s3, r3, s4, r4, kgb, r5, s6, r6, s7, r7,
    hs, hr, sx, rx, sy, ry,
):
    gx = lax.axis_index("gx")
    gy = lax.axis_index("gy")

    def around(i, k):
        return lax.rem(i + k + PEERS, PEERS)

    barrier = pltpu.get_barrier_semaphore()

    @pl.loop(1, PEERS)
    def _(k):
        pl.semaphore_signal(barrier, inc=1, device_id=(around(gx, k), gy), device_id_type=MESH)
        pl.semaphore_signal(barrier, inc=1, device_id=(gx, around(gy, k)), device_id_type=MESH)

    for i in (-1, 1):
        for j in (-1, 1):
            pl.semaphore_signal(
                barrier, inc=1, device_id=(around(gx, i), around(gy, j)), device_id_type=MESH
            )

    sides = [(i, j) for i in (-1, 0, 1) for j in (-1, 0, 1) if (i, j) != (0, 0)]
    x_from = {-1: (2, 2), 0: (2, 4), 1: (4, 2)}
    x_to = {-1: (6, 2), 0: (2, 4), 1: (0, 2)}
    y_from = {-1: (1, 1), 0: (1, 4), 1: (4, 1)}
    y_to = {-1: (5, 1), 0: (1, 4), 1: (0, 1)}

    def rim_copy(ext, which, n, i, j):
        return pltpu.make_async_remote_copy(
            src_ref=ext.at[pl.ds(*x_from[i]), pl.ds(*y_from[j])],
            dst_ref=ext.at[pl.ds(*x_to[i]), pl.ds(*y_to[j])],
            send_sem=hs.at[which, n],
            recv_sem=hr.at[which, n],
            device_id=(around(gx, i), around(gy, j)),
            device_id_type=MESH,
        )

    def rim_send(ext, which):
        for n, (i, j) in enumerate(sides):
            rim_copy(ext, which, n, i, j).start()

    def rim_wait(ext, which):
        for n, (i, j) in enumerate(sides):
            rim_copy(ext, which, n, i, j).wait_recv()

    def rim_done(ext, which):
        for n, (i, j) in enumerate(sides):
            rim_copy(ext, which, n, i, j).wait_send()

    def peer_copy(axis, src, src_at, dst, dst_at, send, recv, which, k, peer):
        return pltpu.make_async_remote_copy(
            src_ref=src.at[pl.ds(src_at, 3)],
            dst_ref=dst.at[pl.ds(dst_at, 3)],
            send_sem=send.at[which, k],
            recv_sem=recv.at[which, k],
            device_id=(peer, gy) if axis == "gx" else (gx, peer),
            device_id_type=MESH,
        )

    def exchange(axis, src, dst, which, scatter):
        me = gx if axis == "gx" else gy
        send, recv = (sx, rx) if axis == "gx" else (sy, ry)

        def start(k):
            peer = around(me, k)
            at = 3 * peer if scatter else 0
            peer_copy(axis, src, at, dst, 3 * me, send, recv, which, k, peer).start()

        def arrived(k):
            peer = around(me, -k)
            at = 3 * peer if scatter else 0
            peer_copy(axis, src, at, dst, 3 * peer, send, recv, which, k, peer).wait_recv()

        def done():
            @pl.loop(1, PEERS)
            def _(k):
                peer = around(me, k)
                at = 3 * peer if scatter else 0
                peer_copy(axis, src, at, dst, 3 * me, send, recv, which, k, peer).wait_send()

        return start, arrived, done

    def start_all(start):
        @pl.loop(1, PEERS)
        def _(k):
            start(k)

    def wait_all(arrived):
        @pl.loop(1, PEERS)
        def _(k):
            arrived(k)

    def total_of(dst, shape):
        def add(k, acc):
            return acc + dst[pl.ds(3 * k, 3)].astype(F32)

        return lax.fori_loop(0, PEERS, add, jnp.zeros(shape, F32))

    def z_modes(rows):
        modes = dot(rows, mz[0]) + dot(rows, mz[1])
        for h in range(2):
            zt[h] = modes[:, 256 * h : 256 * h + 256].reshape(LX, LY, 256)

    def x_send(which):
        start, arrived, done = exchange("gx", s1.at[which], r1.at[which], which, True)

        def units(peer):
            for j in range(3):
                unit = 3 * peer + j
                ix = unit // 2
                half = lax.rem(unit, 2)
                re = jnp.zeros((LY, 128), F32)
                im = jnp.zeros((LY, 128), F32)
                for x in range(LX):
                    c = tx[gx, ix * 8 + 2 * x]
                    s = tx[gx, ix * 8 + 2 * x + 1]
                    zr = zt[half, x, :, 0:128]
                    zi = zt[half, x, :, 128:256]
                    re = re + (c * zr + s * zi)
                    im = im + (c * zi - s * zr)
                s1[which, unit] = jnp.concatenate([re, im], axis=0).astype(BF16)

        @pl.loop(1, PEERS)
        def _(k):
            units(around(gx, k))
            start(k)

        units(gx)
        r1[which, pl.ds(3 * gx, 3)] = s1[which, pl.ds(3 * gx, 3)]
        return arrived, done

    lane = lax.broadcasted_iota(jnp.int32, (LY, 128), 1)

    def y_send(which):
        part = total_of(r1.at[which], (3, 16, 128))
        blocks = []
        for u in range(3):
            re = part[u, 0:8]
            im = part[u, 8:16]
            for k in range(4):
                here = (128 - 32 * k) % 128
                after = (160 - 32 * k) % 128
                re_here = pltpu.roll(re, here, 1) if here else re
                im_here = pltpu.roll(im, here, 1) if here else im
                re_after = pltpu.roll(re, after, 1) if after else re
                im_after = pltpu.roll(im, after, 1) if after else im
                straight = jnp.where(lane < 32, re_here, jnp.where(lane < 64, im_after, 0.0))
                crossed = jnp.where(lane < 32, im_here, jnp.where(lane < 64, -re_after, 0.0))
                blocks.append(jnp.concatenate([straight, crossed], axis=0))
        modes = dot(ty[gy], jnp.concatenate(blocks, axis=1), HIGH)
        for p in range(12):
            s2[which, 4 * p : 4 * p + 4] = modes[:, 128 * p : 128 * p + 128].reshape(4, 8, 128)
        start, arrived, done = exchange("gy", s2.at[which], r2.at[which], 2 * which, True)
        start_all(start)
        r2[which, pl.ds(3 * gy, 3)] = s2[which, pl.ds(3 * gy, 3)]
        return arrived, done

    def modes_send(which):
        start, arrived, done = exchange("gy", s3.at[which], r3.at[which], 2 * which + 1, False)
        start_all(start)
        r3[which, pl.ds(3 * gy, 3)] = s3[which]
        return arrived, done

    def columns_send(which):
        blocks = [r3[which, 4 * p : 4 * p + 4].reshape(32, 128) for p in range(12)]
        cells = dot(tys[gy], jnp.concatenate(blocks, axis=1), HIGH)
        for u in range(3):
            re = jnp.zeros((LY, 128), F32)
            im = jnp.zeros((LY, 128), F32)
            for k in range(4):
                at = 128 * (4 * u + k)
                both = cells[0:8, at : at + 128] + pltpu.roll(cells[8:16, at : at + 128], 64, 1)
                mine = lane // 32 == k
                up = 32 * k
                down = (32 * k + 96) % 128
                re = jnp.where(mine, pltpu.roll(both, up, 1) if up else both, re)
                im = jnp.where(mine, pltpu.roll(both, down, 1) if down else both, im)
            s4[which, u] = jnp.concatenate([re, im], axis=0).astype(BF16)
        start, arrived, done = exchange("gx", s4.at[which], r4.at[which], 2 + which, False)
        start_all(start)
        r4[which, pl.ds(3 * gx, 3)] = s4[which]
        return arrived, done

    def cells_of(which):
        def step(jj, acc):
            acc = list(acc)
            for t in range(3):
                ix = 3 * jj + t
                for h in range(2):
                    unit = r4[which, 6 * jj + 2 * t + h].astype(F32)
                    re = unit[0:8]
                    im = unit[8:16]
                    for x in range(LX):
                        c = tx[gx, ix * 8 + 2 * x]
                        s = tx[gx, ix * 8 + 2 * x + 1]
                        at = (h * LX + x) * 2
                        acc[at] = acc[at] + (c * re - s * im)
                        acc[at + 1] = acc[at + 1] + (c * im + s * re)
            return tuple(acc)

        zero = jnp.zeros((LY, 128), F32)
        acc = lax.fori_loop(0, 8, step, (zero,) * 16)
        rows = [
            jnp.concatenate([acc[x * 2], acc[x * 2 + 1], acc[8 + x * 2], acc[9 + x * 2]], axis=1)
            for x in range(LX)
        ]
        modes = jnp.concatenate(rows, axis=0)
        high = modes.astype(BF16)
        low = (modes - high.astype(F32)).astype(BF16)
        return dot(high, mzs[0]) + (dot(high, mzs[1]) + dot(low, mzs[0]))

    def windows(dst, values):
        n = values.shape[0]
        zb = lax.broadcasted_iota(jnp.int32, (n, 8, 128), 1)
        ln = lax.broadcasted_iota(jnp.int32, (n, 8, 128), 2)
        before = pltpu.roll(values, 1, 1)
        after = pltpu.roll(values, 7, 1)
        edge = jnp.where(
            (ln >= 96) & (zb > 0), before, jnp.where((ln < 32) & (zb < 7), after, 0.0)
        )
        dst[:, :, 0:128] = values
        dst[:, :, 128:256] = edge

    def conv(src, kernel, nx, ny, acc):
        acc[...] = jnp.zeros_like(acc)

        @pl.loop(0, 9)
        def _(ab):
            a = ab // 3
            b = lax.rem(ab, 3)
            rows = src[pl.ds(a, nx), pl.ds(b, ny)].reshape(nx * ny * 8, 256).astype(BF16)
            acc[...] += dot(rows, band[kernel, ab])

    def correlate(src, off, grad, q):
        turned = grad.T.astype(BF16)

        @pl.loop(0, 9)
        def _(ab):
            a = ab // 3 + off
            b = lax.rem(ab, 3) + off
            rows = src[pl.ds(a, LX), pl.ds(b, LY)].reshape(256, 256).astype(BF16)
            prod = dot(turned, rows)
            acc = jnp.zeros((C, 256), F32)
            for zl in range(4):
                shift = (32 - 32 * zl) % 256
                piece = prod[32 * zl : 32 * zl + 32]
                acc = acc + (pltpu.roll(piece, shift, 1) if shift else piece)
            tile = acc[:, 0:128].astype(BF16)
            kgb[(q * 9 + ab) * 2] = tile[0:16]
            kgb[(q * 9 + ab) * 2 + 1] = tile[16:32]

    def widen(ext, dst):
        @pl.loop(0, 8)
        def _(i):
            values = ext[i].astype(F32).reshape(12, 8, 128)
            yi = lax.broadcasted_iota(jnp.int32, (12, 8, 128), 0) + (gy * LY - 2)
            row = gx * LX - 2 + i
            ok = (row >= 0) & (row < NX) & (yi >= 0) & (yi < NY)
            windows(dst.at[i], jnp.where(ok, values, 0.0))

    for x in range(LX):
        mine = field[x].astype(F32)
        g = cot[x].astype(F32)
        for b in range(8):
            sp[8 * x : 8 * x + 8, b, :] = mine[:, 128 * b : 128 * b + 128]
            cg[8 * x : 8 * x + 8, b, :] = g[:, 128 * b : 128 * b + 128]
    xe[2:6, 1:5] = sp[...].reshape(4, 4, 16, 128).astype(BF16)
    z_modes(field[...].reshape(32, 1024))

    pl.semaphore_wait(barrier, 2 * (PEERS - 1) + 4)

    rim_send(xe, 0)
    x_arrived, x_done = x_send(0)

    group = lax.broadcasted_iota(jnp.int32, (C, 128), 1) // C
    for q in range(4):

        @pl.loop(0, 9)
        def _(ab):
            taps = [kk[q, 3 * ab + e].astype(F32) for e in range(3)]
            for block in range(8):
                z = block if block < 5 else block - 8
                rows = jnp.zeros((C, 128), F32)
                for e in range(3):
                    if 0 <= z + 1 - e < 4:
                        rows = jnp.where(group == z + 1 - e, taps[e], rows)
                band[q, ab, 32 * block : 32 * block + 32] = rows.astype(BF16)

    kgb[36:48] = jnp.zeros((12, 16, 128), BF16)

    rim_wait(xe, 0)
    widen(xe, xw)
    conv(xw, 0, 6, 10, pre)

    wait_all(x_arrived)
    y_arrived, y_done = y_send(0)

    @pl.loop(0, 6)
    def _(i):
        rows = pl.ds(pl.multiple_of(i * 80, 80), 80)
        h, slope = gelu_parts(pre[rows])
        pre[rows] = slope
        yi = lax.broadcasted_iota(jnp.int32, (10, 8, 128), 0) + (gy * LY - 1)
        row = gx * LX - 1 + i
        ok = (row >= 0) & (row < NX) & (yi >= 0) & (yi < NY)
        h = h.astype(BF16).astype(F32).reshape(10, 8, 128)
        windows(hw.at[i], jnp.where(ok, h, 0.0))

    conv(hw, 1, 4, 8, brn)

    wait_all(y_arrived)
    first = (gx * PEERS + gy) * 18

    def scale_of(m):
        kz = lax.rem((first + m) // MY, MZ)
        return jnp.where(kz == 0, 1.0 / (NX * NY * NZ), 2.0 / (NX * NY * NZ)).astype(F32)

    spectrum = total_of(r2.at[0], (3, 8, 128)).reshape(24, 128)
    xt[...] = jnp.concatenate([spectrum, jnp.zeros((104, 128), F32)], axis=0).T
    s3[...] = jnp.zeros_like(s3)
    for m in range(18):
        j, row = divmod(m, 6)
        at = 8 * j + row
        xr = xt[0:32, at : at + 1]
        xi = xt[32:64, at : at + 1]
        wr = sw[0, m]
        wi = sw[1, m]
        sc = scale_of(m)
        yr = jnp.sum(xr * wr - xi * wi, axis=0, keepdims=True) * sc
        yi = jnp.sum(xr * wi + xi * wr, axis=0, keepdims=True) * sc
        s3[0, j, row : row + 1, :] = jnp.concatenate([yr, yi, -yi, yr], axis=1)
    m_arrived, m_done = modes_send(0)
    wait_all(m_arrived)
    c_arrived, c_done = columns_send(0)
    wait_all(c_arrived)
    spectral = cells_of(0)
    for b in range(8):
        sp[:, b, :] = spectral[:, 128 * b : 128 * b + 128]

    _, slope = gelu_parts(sp[...].reshape(256, 128) + brn[...])
    dtotal = (cg[...].reshape(256, 128) * slope).astype(BF16)
    de[2:6, 1:5] = dtotal.reshape(4, 4, 16, 128)
    rim_send(de, 1)
    dts[...] = dtotal.astype(F32).reshape(32, 8, 128)
    for b in range(8):
        dtl[:, 128 * b : 128 * b + 128] = dts[:, b, :].astype(BF16)
    z_modes(dtl[...])
    x_arrived2, x_done2 = x_send(1)

    correlate(hw, 0, dts[...].reshape(256, 128), 1)
    rim_wait(de, 1)
    widen(de, dw)

    wait_all(x_arrived2)
    y_arrived2, y_done2 = y_send(1)

    conv_ext(dw, 2, pre, pw, band, gx, gy, windows)

    wait_all(y_arrived2)
    grads = total_of(r2.at[1], (3, 8, 128))
    mode_lane = lax.broadcasted_iota(jnp.int32, (128, 128), 1)
    back = jnp.zeros((128, 128), F32)
    for m in range(18):
        j, row = divmod(m, 6)
        at = 8 * j + row
        xr = xt[0:32, at : at + 1]
        xi = xt[32:64, at : at + 1]
        wr = sw[0, m]
        wi = sw[1, m]
        dy = grads[j, row : row + 1, :] * scale_of(m)
        dyr = dy[:, 0:32]
        dyi = dy[:, 32:64]
        out_sg[0, m] = xr * dyr + xi * dyi
        out_sg[1, m] = xr * dyi - xi * dyr
        dxr = jnp.sum(wr * dyr + wi * dyi, axis=1, keepdims=True)
        dxi = jnp.sum(wr * dyi - wi * dyr, axis=1, keepdims=True)
        column = jnp.concatenate([dxr, dxi, -dxi, dxr], axis=0)
        back = jnp.where(mode_lane == at, column, back)
    s3[1] = back.T[0:24].reshape(3, 8, 128)
    m_arrived2, m_done2 = modes_send(1)

    correlate(xw, 1, pw[1:5, 1:9, :, 0:128].reshape(256, 128), 0)
    k_start, k_arrived, k_done = exchange("gx", kgb, r5, 4, True)
    start_all(k_start)
    r5[pl.ds(3 * gx, 3)] = kgb[pl.ds(3 * gx, 3)]

    wait_all(m_arrived2)
    c_arrived2, c_done2 = columns_send(1)

    conv(pw, 3, 4, 8, brn)
    wait_all(k_arrived)
    s6[...] = total_of(r5, (3, 16, 128))
    l_start, l_arrived, l_done = exchange("gy", s6, r6, 4, False)
    start_all(l_start)
    r6[pl.ds(3 * gy, 3)] = s6[...]

    wait_all(c_arrived2)
    spectral = cells_of(1)
    wait_all(l_arrived)
    s7[...] = total_of(r6, (3, 16, 128))
    n_start, n_arrived, n_done = exchange("gx", s7, r7, 5, False)
    start_all(n_start)
    r7[pl.ds(3 * gx, 3)] = s7[...]

    dts[...] = brn[...].reshape(32, 8, 128)
    for b in range(8):
        value = spectral[:, 128 * b : 128 * b + 128] + dts[:, b, :]
        out_field[:, :, 128 * b : 128 * b + 128] = value.reshape(LX, LY, 128).astype(BF16)
    wait_all(n_arrived)
    out_kg[...] = r7[0:36]

    rim_done(xe, 0)
    rim_done(de, 1)
    for done in (
        x_done, y_done, m_done, c_done, x_done2, y_done2, m_done2, c_done2, k_done, l_done, n_done
    ):
        done()


def conv_ext(dw, kernel, slope, pw, band, gx, gy, windows):
    @pl.loop(0, 6)
    def _(i):
        def tap(ab, acc):
            a = ab // 3
            b = lax.rem(ab, 3)
            rows = dw[i + a, pl.ds(b, 10)].reshape(80, 256).astype(BF16)
            return acc + dot(rows, band[kernel, ab])

        dhidden = lax.fori_loop(0, 9, tap, jnp.zeros((80, 128), F32))
        rows = pl.ds(pl.multiple_of(i * 80, 80), 80)
        dpre = (dhidden * slope[rows]).astype(BF16).astype(F32).reshape(10, 8, 128)
        yi = lax.broadcasted_iota(jnp.int32, (10, 8, 128), 0) + (gy * LY - 1)
        row = gx * LX - 1 + i
        ok = (row >= 0) & (row < NX) & (yi >= 0) & (yi < NY)
        windows(pw.at[i], jnp.where(ok, dpre, 0.0))


def shards(field, cotangent, kernel_one, kernel_two, spectral_weight):
    mz, mzs, tx, ty, tys = constants()
    back_two = kernel_two[::-1].transpose(0, 2, 1)
    back_one = kernel_one[::-1].transpose(0, 2, 1)
    kk = jnp.tile(jnp.stack([kernel_one, kernel_two, back_two, back_one]), (1, 1, 1, 4))
    vmem = pl.BlockSpec(memory_space=pltpu.VMEM)
    smem = pl.BlockSpec(memory_space=pltpu.SMEM)

    def buf(shape, dtype=F32):
        return pltpu.VMEM(shape, dtype)

    field_grad, kg, sg = pl.pallas_call(
        body,
        out_shape=(
            jax.ShapeDtypeStruct((LX, LY, NZ * C), BF16),
            jax.ShapeDtypeStruct((36, 16, 128), F32),
            jax.ShapeDtypeStruct(spectral_weight.shape, F32),
        ),
        in_specs=[vmem, vmem, vmem, vmem, vmem, vmem, smem, vmem, vmem],
        out_specs=(vmem, vmem, vmem),
        scratch_shapes=[
            buf((8, 6, 16, 128), BF16),
            buf((8, 6, 16, 128), BF16),
            buf((8, 12, 8, 256)),
            buf((6, 10, 8, 256)),
            buf((8, 12, 8, 256)),
            buf((6, 10, 8, 256)),
            buf((480, 128)),
            buf((256, 128)),
            buf((4, 9, 256, 128), BF16),
            buf((32, 8, 128)),
            buf((2, LX, LY, 256)),
            buf((32, 8, 128)),
            buf((32, 8, 128)),
            buf((32, 1024), BF16),
            buf((2, 48, 16, 128), BF16),
            buf((2, 48, 16, 128), BF16),
            buf((2, 48, 8, 128)),
            buf((2, 48, 8, 128)),
            buf((128, 128)),
            buf((2, 3, 8, 128)),
            buf((2, 48, 8, 128)),
            buf((2, 3, 16, 128), BF16),
            buf((2, 48, 16, 128), BF16),
            buf((48, 16, 128), BF16),
            buf((48, 16, 128), BF16),
            buf((3, 16, 128)),
            buf((48, 16, 128)),
            buf((3, 16, 128)),
            buf((48, 16, 128)),
            pltpu.SemaphoreType.DMA((2, 8)),
            pltpu.SemaphoreType.DMA((2, 8)),
            pltpu.SemaphoreType.DMA((6, PEERS)),
            pltpu.SemaphoreType.DMA((6, PEERS)),
            pltpu.SemaphoreType.DMA((5, PEERS)),
            pltpu.SemaphoreType.DMA((5, PEERS)),
        ],
        compiler_params=pltpu.CompilerParams(
            collective_id=0, has_side_effects=True, vmem_limit_bytes=56 << 20
        ),
    )(field, cotangent, kk, spectral_weight, mz, mzs, tx, ty, tys)
    kg = kg.reshape(2, 9, C, 128)[..., : 3 * C].reshape(2, 9, C, 3, C)
    kg = kg.transpose(0, 1, 3, 4, 2).reshape(2, 27, C, C)
    return (field_grad, kg[0], kg[1], sg)


def solution(mesh):
    return jax.shard_map(
        shards,
        mesh=mesh,
        in_specs=(
            P("gx", "gy", None),
            P("gx", "gy", None),
            P(),
            P(),
            P(None, ("gx", "gy"), None, None),
        ),
        out_specs=(P("gx", "gy", None), P(), P(), P(None, ("gx", "gy"), None, None)),
        check_vma=False,
    )
```

```python
import math

import jax
import jax.numpy as jnp
import numpy as np
from jax import lax
from jax.experimental import pallas as pl
from jax.experimental.pallas import tpu as pltpu
from jax.sharding import PartitionSpec as P

C = 32
MX = 24
MY = 24
MZ = 8
NZ = 32
NX = 64
NY = 128
PEERS = 16
LX = 4
LY = 8
MESH = pl.DeviceIdType.MESH
F32 = jnp.float32
BF16 = jnp.bfloat16
HIGH = lax.Precision.HIGHEST


def kept(length, count):
    half = count // 2
    return np.concatenate([np.arange(half), length - half + np.arange(half)])


def angles(coords, freqs, length):
    return (coords[:, None] * freqs[None, :] % length) * (2.0 * math.pi / length)


def split(table):
    high = table.astype(BF16)
    low = (table - high.astype(np.float64)).astype(BF16)
    return np.stack([high, low])


def constants():
    az = angles(np.arange(NZ), np.arange(MZ), NZ).reshape(NZ, 2, 4)
    fz = np.stack([np.cos(az), -np.sin(az)], axis=2)
    mz = np.einsum("zhrk,ij->zihrkj", fz, np.eye(C)).reshape(NZ * C, 2 * MZ * C)
    ax = angles(np.arange(NX), kept(NX, MX), NX)
    tx = np.stack([np.cos(ax), np.sin(ax)], axis=-1).reshape(PEERS, LX, MX, 2)
    tx = tx.transpose(0, 2, 1, 3).reshape(PEERS, MX * LX * 2)
    ay = angles(np.arange(NY), kept(NY, MY), NY).reshape(PEERS, LY, 12, 2)
    cy = np.zeros((PEERS, 2, 16, LY))
    sy = np.zeros((PEERS, 2, 16, LY))
    cy[:, :, :12] = np.cos(ay).transpose(0, 3, 2, 1)
    sy[:, :, :12] = np.sin(ay).transpose(0, 3, 2, 1)
    ty = np.concatenate([cy, sy], axis=3).reshape(PEERS, 32, 16)
    tys = np.stack([cy, sy], axis=1).transpose(0, 1, 2, 4, 3).reshape(PEERS, 32, 16)
    return (
        split(mz),
        split(mz.T),
        tx.astype(np.float32),
        ty.astype(np.float32),
        tys.astype(np.float32),
    )


def gelu_parts(x):
    k = math.sqrt(2.0 / math.pi)
    t = jnp.tanh(k * (x + 0.044715 * (x * x * x)))
    cdf = 0.5 * (1.0 + t)
    slope = cdf + x * (0.5 * (1.0 - t * t)) * (k * (1.0 + (3.0 * 0.044715) * (x * x)))
    return x * cdf, slope


def dot(a, b, precision=None):
    return jnp.dot(a, b, preferred_element_type=F32, precision=precision)


def body(
    field, cot, k1, k2, sw_hbm, mz_hbm, mzs_hbm, tx, ty, tys,
    out_field, out_k1, out_k2, out_sg,
    sw, mz, mzs, taps, wide,
    xe, de, xw, hw, dw, pw, pre, brn, band, cg, zt, sp, dts, dtl,
    s1, r1, s2, r2, xs, xt, yf, yg, s3, r3, s4, r4, kgf, kgb, r5, s6, r6, s7, r7,
    hs, hr, sx, rx, sy, ry, ls,
):
    load_z = pltpu.make_async_copy(mz_hbm, mz, ls.at[0])
    load_w = pltpu.make_async_copy(sw_hbm, sw, ls.at[1])
    load_zs = pltpu.make_async_copy(mzs_hbm, mzs, ls.at[2])
    load_z.start()
    load_w.start()
    load_zs.start()
    gx = lax.axis_index("gx")
    gy = lax.axis_index("gy")

    def around(i, k):
        return lax.rem(i + k + PEERS, PEERS)

    barrier = pltpu.get_barrier_semaphore()

    @pl.loop(1, PEERS)
    def _(k):
        pl.semaphore_signal(barrier, inc=1, device_id=(around(gx, k), gy), device_id_type=MESH)
        pl.semaphore_signal(barrier, inc=1, device_id=(gx, around(gy, k)), device_id_type=MESH)

    for i in (-1, 1):
        for j in (-1, 1):
            pl.semaphore_signal(
                barrier, inc=1, device_id=(around(gx, i), around(gy, j)), device_id_type=MESH
            )

    sides = [(i, j) for i in (-1, 0, 1) for j in (-1, 0, 1) if (i, j) != (0, 0)]
    x_from = {-1: (2, 2), 0: (2, 4), 1: (4, 2)}
    x_to = {-1: (6, 2), 0: (2, 4), 1: (0, 2)}
    y_from = {-1: (1, 1), 0: (1, 4), 1: (4, 1)}
    y_to = {-1: (5, 1), 0: (1, 4), 1: (0, 1)}

    def rim_copy(ext, which, n, i, j):
        return pltpu.make_async_remote_copy(
            src_ref=ext.at[pl.ds(*x_from[i]), pl.ds(*y_from[j])],
            dst_ref=ext.at[pl.ds(*x_to[i]), pl.ds(*y_to[j])],
            send_sem=hs.at[which, n],
            recv_sem=hr.at[which, n],
            device_id=(around(gx, i), around(gy, j)),
            device_id_type=MESH,
        )

    def rim_send(ext, which):
        for n, (i, j) in enumerate(sides):
            rim_copy(ext, which, n, i, j).start()

    def rim_wait(ext, which):
        for n, (i, j) in enumerate(sides):
            rim_copy(ext, which, n, i, j).wait_recv()

    def rim_done(ext, which):
        for n, (i, j) in enumerate(sides):
            rim_copy(ext, which, n, i, j).wait_send()

    def exchange(axis, src, dst, which, scatter, n):
        me = gx if axis == "gx" else gy
        send, recv = (sx, rx) if axis == "gx" else (sy, ry)

        def copy(k, peer, slot):
            return pltpu.make_async_remote_copy(
                src_ref=src.at[pl.ds(n * peer if scatter else 0, n)],
                dst_ref=dst.at[pl.ds(n * slot, n)],
                send_sem=send.at[which, k],
                recv_sem=recv.at[which, k],
                device_id=(peer, gy) if axis == "gx" else (gx, peer),
                device_id_type=MESH,
            )

        def start(k):
            copy(k, around(me, k), me).start()

        def arrived(k):
            peer = around(me, -k)
            copy(k, peer, peer).wait_recv()

        def done():
            @pl.loop(1, PEERS)
            def _(k):
                copy(k, around(me, k), me).wait_send()

        return start, arrived, done

    def start_all(start):
        @pl.loop(1, PEERS)
        def _(k):
            start(k)

    def wait_all(arrived):
        @pl.loop(1, PEERS)
        def _(k):
            arrived(k)

    def total_of(dst, n):
        def add(k, acc):
            return acc + dst[pl.ds(n * k, n)].astype(F32)

        return lax.fori_loop(0, PEERS, add, jnp.zeros((n,) + dst.shape[1:], F32))

    def z_modes(rows):
        modes = dot(rows, mz[0]) + dot(rows, mz[1])
        for h in range(2):
            zt[h] = modes[:, 256 * h : 256 * h + 256].reshape(LX, LY, 256)

    def x_send(which):
        start, arrived, done = exchange("gx", s1.at[which], r1.at[which], which, True, 3)

        def units(peer):
            for j in range(3):
                unit = 3 * peer + j
                ix = unit // 2
                half = lax.rem(unit, 2)
                re = jnp.zeros((LY, 128), F32)
                im = jnp.zeros((LY, 128), F32)
                for x in range(LX):
                    c = tx[gx, ix * 8 + 2 * x]
                    s = tx[gx, ix * 8 + 2 * x + 1]
                    zr = zt[half, x, :, 0:128]
                    zi = zt[half, x, :, 128:256]
                    re = re + (c * zr + s * zi)
                    im = im + (c * zi - s * zr)
                s1[which, unit] = jnp.concatenate([re, im], axis=0).astype(BF16)

        @pl.loop(1, PEERS)
        def _(k):
            units(around(gx, k))
            start(k)

        units(gx)
        r1[which, pl.ds(3 * gx, 3)] = s1[which, pl.ds(3 * gx, 3)]
        return arrived, done

    lane = lax.broadcasted_iota(jnp.int32, (LY, 128), 1)

    def y_send(which):
        part = total_of(r1.at[which], 3)
        blocks = []
        for u in range(3):
            re = part[u, 0:8]
            im = part[u, 8:16]
            for k in range(4):
                here = (128 - 32 * k) % 128
                after = (160 - 32 * k) % 128
                re_here = pltpu.roll(re, here, 1) if here else re
                im_here = pltpu.roll(im, here, 1) if here else im
                re_after = pltpu.roll(re, after, 1) if after else re
                im_after = pltpu.roll(im, after, 1) if after else im
                straight = jnp.where(lane < 32, re_here, jnp.where(lane < 64, im_after, 0.0))
                crossed = jnp.where(lane < 32, im_here, jnp.where(lane < 64, -re_after, 0.0))
                blocks.append(jnp.concatenate([straight, crossed], axis=0))
        modes = dot(ty[gy], jnp.concatenate(blocks, axis=1), HIGH)
        for p in range(12):
            at = 128 * p
            rows = modes[0:16, at : at + 128] + pltpu.roll(modes[16:32, at : at + 128], 64, 1)
            yf[12 * p : 12 * p + 12] = rows[0:12]
        for d in range(PEERS):
            s2[which, d] = yf[9 * d : 9 * d + 9]
        start, arrived, done = exchange("gy", s2.at[which], r2.at[which], 2 * which, True, 1)
        start_all(start)
        r2[which, gy] = s2[which, gy]
        return arrived, done

    def modes_send(which):
        start, arrived, done = exchange("gy", s3.at[which], r3.at[which], 2 * which + 1, False, 1)
        start_all(start)
        r3[which, gy] = s3[which, 0]
        return arrived, done

    def columns_send(which):
        for d in range(PEERS):
            row = 9 * d
            while row < 9 * d + 9:
                p = row // 12
                end = min(9 * d + 9, 12 * p + 12)
                yg[p, row - 12 * p : end - 12 * p] = r3[which, d, row - 9 * d : end - 9 * d]
                row = end
        cells = dot(tys[gy], jnp.concatenate([yg[p] for p in range(12)], axis=1), HIGH)
        for u in range(3):
            re = jnp.zeros((LY, 128), F32)
            im = jnp.zeros((LY, 128), F32)
            for k in range(4):
                at = 128 * (4 * u + k)
                cell = cells[:, at : at + 128]
                cosine = cell[0:8] + pltpu.roll(cell[8:16], 64, 1)
                sine = cell[16:24] + pltpu.roll(cell[24:32], 64, 1)
                both = cosine + jnp.where(
                    lane < 32, -pltpu.roll(sine, 96, 1), pltpu.roll(sine, 32, 1)
                )
                mine = lane // 32 == k
                up = 32 * k
                down = (32 * k + 96) % 128
                re = jnp.where(mine, pltpu.roll(both, up, 1) if up else both, re)
                im = jnp.where(mine, pltpu.roll(both, down, 1) if down else both, im)
            s4[which, u] = jnp.concatenate([re, im], axis=0).astype(BF16)
        start, arrived, done = exchange("gx", s4.at[which], r4.at[which], 2 + which, False, 3)
        start_all(start)
        r4[which, pl.ds(3 * gx, 3)] = s4[which]
        return arrived, done

    def cells_of(which):
        def step(jj, acc):
            acc = list(acc)
            for t in range(3):
                ix = 3 * jj + t
                for h in range(2):
                    unit = r4[which, 6 * jj + 2 * t + h].astype(F32)
                    re = unit[0:8]
                    im = unit[8:16]
                    for x in range(LX):
                        c = tx[gx, ix * 8 + 2 * x]
                        s = tx[gx, ix * 8 + 2 * x + 1]
                        at = (h * LX + x) * 2
                        acc[at] = acc[at] + (c * re - s * im)
                        acc[at + 1] = acc[at + 1] + (c * im + s * re)
            return tuple(acc)

        zero = jnp.zeros((LY, 128), F32)
        acc = lax.fori_loop(0, 8, step, (zero,) * 16)
        rows = [
            jnp.concatenate([acc[x * 2], acc[x * 2 + 1], acc[8 + x * 2], acc[9 + x * 2]], axis=1)
            for x in range(LX)
        ]
        modes = jnp.concatenate(rows, axis=0)
        high = modes.astype(BF16)
        low = (modes - high.astype(F32)).astype(BF16)
        return dot(high, mzs[0]) + (dot(high, mzs[1]) + dot(low, mzs[0]))

    def windows(dst, i, values):
        n = values.shape[0]
        zb = lax.broadcasted_iota(jnp.int32, (n, 8, 128), 1)
        ln = lax.broadcasted_iota(jnp.int32, (n, 8, 128), 2)
        before = pltpu.roll(values, 1, 1)
        after = pltpu.roll(values, 7, 1)
        edge = jnp.where(
            (ln >= 96) & (zb > 0), before, jnp.where((ln < 32) & (zb < 7), after, 0.0)
        )
        for part, lanes in ((values, 0), (edge, 128)):
            even = part.reshape(n // 2, 16, 128).astype(BF16)
            odd = part[1 : n - 1].reshape(n // 2 - 1, 16, 128).astype(BF16)
            dst[0, i, :, :, lanes : lanes + 128] = even
            dst[1, i, 0 : n // 2 - 1, :, lanes : lanes + 128] = odd

    def conv(src, kernel, nx, ny, acc):
        total = jnp.zeros((nx * ny * 8, 128), F32)
        for ab in range(9):
            a, b = divmod(ab, 3)
            rows = src[b % 2, a : a + nx, b // 2 : b // 2 + ny // 2].reshape(nx * ny * 8, 256)
            total = total + dot(rows, band[kernel, ab])
        acc[...] = total

    def correlate(src, off, grad, q):
        turned = grad.T.astype(BF16)

        lanes = lax.broadcasted_iota(jnp.int32, (C, 256), 1)
        for ab in range(9):
            a, b = divmod(ab, 3)
            a, b = a + off, b + off
            rows = src[b % 2, a : a + LX, b // 2 : b // 2 + LY // 2].reshape(256, 256)
            prod = dot(turned, rows)
            group, place = divmod((q * 9 + ab) * 3, 4)
            first_lane = 32 * place
            acc = jnp.zeros((C, 256), F32)
            for zl in range(4):
                shift = (32 - 32 * zl + first_lane) % 256
                piece = prod[32 * zl : 32 * zl + 32]
                acc = acc + (pltpu.roll(piece, shift, 1) if shift else piece)
            acc = jnp.where((lanes >= first_lane) & (lanes < first_lane + 96), acc, 0.0)
            kgf[32 * group : 32 * group + 32] += acc[:, 0:128]
            if first_lane + 96 > 128:
                kgf[32 * group + 32 : 32 * group + 64] += acc[:, 128:256]

    def widen(ext, dst):
        @pl.loop(0, 8)
        def _(i):
            values = ext[i].astype(F32).reshape(12, 8, 128)
            yi = lax.broadcasted_iota(jnp.int32, (12, 8, 128), 0) + (gy * LY - 2)
            row = gx * LX - 2 + i
            ok = (row >= 0) & (row < NX) & (yi >= 0) & (yi < NY)
            windows(dst, i, jnp.where(ok, values, 0.0))

    for x in range(LX):
        mine = field[x].astype(F32)
        g = cot[x].astype(F32)
        for b in range(8):
            sp[8 * x : 8 * x + 8, b, :] = mine[:, 128 * b : 128 * b + 128]
            cg[8 * x : 8 * x + 8, b, :] = g[:, 128 * b : 128 * b + 128]
    xe[2:6, 1:5] = sp[...].reshape(4, 4, 16, 128).astype(BF16)
    load_z.wait()
    z_modes(field[...].reshape(32, 1024))

    pl.semaphore_wait(barrier, 2 * (PEERS - 1) + 4)

    x_arrived, x_done = x_send(0)
    rim_send(xe, 0)

    group = lax.broadcasted_iota(jnp.int32, (C, 128), 1) // C
    for q, kernel in ((0, k1), (1, k2)):

        @pl.loop(0, 9)
        def _(ab):
            wide = []
            for e in range(3):
                tap = kernel[3 * ab + e].astype(F32)
                wide.append(jnp.concatenate([tap] * 4, axis=1))
            for block in range(8):
                z = block if block < 5 else block - 8
                rows = jnp.zeros((C, 128), F32)
                for e in range(3):
                    if 0 <= z + 1 - e < 4:
                        rows = jnp.where(group == z + 1 - e, wide[e], rows)
                taps[32 * block : 32 * block + 32] = rows
            band[q, ab] = taps[...].astype(BF16)
            band[3 - q, 8 - ab, 0:128] = taps[0:128].T.astype(BF16)
            band[3 - q, 8 - ab, 128:256] = taps[128:256].T.astype(BF16)

    kgf[...] = jnp.zeros_like(kgf)
    yg[...] = jnp.zeros_like(yg)

    rim_wait(xe, 0)
    widen(xe, xw)
    conv(xw, 0, 6, 10, pre)

    wait_all(x_arrived)
    y_arrived, y_done = y_send(0)

    @pl.loop(0, 6)
    def _(i):
        rows = pl.ds(pl.multiple_of(i * 80, 80), 80)
        h, slope = gelu_parts(pre[rows])
        pre[rows] = slope
        yi = lax.broadcasted_iota(jnp.int32, (10, 8, 128), 0) + (gy * LY - 1)
        row = gx * LX - 1 + i
        ok = (row >= 0) & (row < NX) & (yi >= 0) & (yi < NY)
        h = h.astype(BF16).astype(F32).reshape(10, 8, 128)
        windows(hw, i, jnp.where(ok, h, 0.0))

    conv(hw, 1, 4, 8, brn)

    wait_all(y_arrived)
    load_w.wait()
    first = (gx * PEERS + gy) * 18

    def scale_of(m):
        kz = lax.rem((first + m) // MY, MZ)
        return jnp.where(kz == 0, 1.0 / (NX * NY * NZ), 2.0 / (NX * NY * NZ)).astype(F32)

    xs[...] = jnp.zeros_like(xs)
    xs[0:9] = total_of(r2.at[0], 1)[0]
    xt[...] = xs[...].T
    for t in range(9):
        row = []
        for half in range(2):
            m = 2 * t + half
            xr = xt[64 * half : 64 * half + 32, t : t + 1]
            xi = xt[64 * half + 32 : 64 * half + 64, t : t + 1]
            wr = sw[0, m]
            wi = sw[1, m]
            row.append(jnp.sum(xr * wr - xi * wi, axis=0, keepdims=True) * scale_of(m))
            row.append(jnp.sum(xr * wi + xi * wr, axis=0, keepdims=True) * scale_of(m))
        s3[0, 0, t : t + 1, :] = jnp.concatenate(row, axis=1)
    m_arrived, m_done = modes_send(0)
    wait_all(m_arrived)
    c_arrived, c_done = columns_send(0)
    load_zs.wait()
    wait_all(c_arrived)
    spectral = cells_of(0)
    for b in range(8):
        sp[:, b, :] = spectral[:, 128 * b : 128 * b + 128]

    _, slope = gelu_parts(sp[...].reshape(256, 128) + brn[...])
    dtotal = (cg[...].reshape(256, 128) * slope).astype(BF16)
    de[2:6, 1:5] = dtotal.reshape(4, 4, 16, 128)
    rim_send(de, 1)
    dts[...] = dtotal.astype(F32).reshape(32, 8, 128)
    for b in range(8):
        dtl[:, 128 * b : 128 * b + 128] = dts[:, b, :].astype(BF16)
    z_modes(dtl[...])
    x_arrived2, x_done2 = x_send(1)

    rim_wait(de, 1)
    widen(de, dw)
    conv(dw, 2, 6, 10, wide)

    @pl.loop(0, 6)
    def _(i):
        rows = pl.ds(pl.multiple_of(i * 80, 80), 80)
        dpre = (wide[rows] * pre[rows]).astype(BF16).astype(F32).reshape(10, 8, 128)
        yi = lax.broadcasted_iota(jnp.int32, (10, 8, 128), 0) + (gy * LY - 1)
        row = gx * LX - 1 + i
        ok = (row >= 0) & (row < NX) & (yi >= 0) & (yi < NY)
        windows(pw, i, jnp.where(ok, dpre, 0.0))

    wait_all(x_arrived2)
    y_arrived2, y_done2 = y_send(1)

    correlate(hw, 0, dts[...].reshape(256, 128), 1)
    correlate(xw, 1, pw[1, 1:5, 0:4, :, 0:128].reshape(256, 128).astype(F32), 0)
    for d in range(PEERS):
        kgb[d] = kgf[28 * d : 28 * d + 32].astype(BF16)
    k_start, k_arrived, k_done = exchange("gx", kgb, r5, 4, True, 1)
    start_all(k_start)
    r5[gx] = kgb[gx]

    wait_all(y_arrived2)
    xs[0:9] = total_of(r2.at[1], 1)[0]
    mode_lane = lax.broadcasted_iota(jnp.int32, (128, 128), 1)
    back = jnp.zeros((128, 128), F32)
    for t in range(9):
        column = []
        for half in range(2):
            m = 2 * t + half
            xr = xt[64 * half : 64 * half + 32, t : t + 1]
            xi = xt[64 * half + 32 : 64 * half + 64, t : t + 1]
            wr = sw[0, m]
            wi = sw[1, m]
            dy = xs[t : t + 1, :] * scale_of(m)
            dyr = dy[:, 64 * half : 64 * half + 32]
            dyi = dy[:, 64 * half + 32 : 64 * half + 64]
            out_sg[0, m] = xr * dyr + xi * dyi
            out_sg[1, m] = xr * dyi - xi * dyr
            column.append(jnp.sum(wr * dyr + wi * dyi, axis=1, keepdims=True))
            column.append(jnp.sum(wr * dyi - wi * dyr, axis=1, keepdims=True))
        back = jnp.where(mode_lane == t, jnp.concatenate(column, axis=0), back)
    xs[...] = back.T
    s3[1, 0] = xs[0:9]
    m_arrived2, m_done2 = modes_send(1)

    wait_all(k_arrived)
    s6[0] = total_of(r5, 1)[0, 0:28]
    l_start, l_arrived, l_done = exchange("gy", s6, r6, 4, False, 1)
    start_all(l_start)
    r6[gy] = s6[0]
    conv(pw, 3, 4, 8, brn)

    wait_all(m_arrived2)
    c_arrived2, c_done2 = columns_send(1)

    wait_all(l_arrived)
    s7[...] = total_of(r6, 1)
    n_start, n_arrived, n_done = exchange("gx", s7, r7, 5, False, 1)
    start_all(n_start)
    r7[gx] = s7[0]

    wait_all(c_arrived2)
    spectral = cells_of(1)
    dts[...] = brn[...].reshape(32, 8, 128)
    for b in range(8):
        value = spectral[:, 128 * b : 128 * b + 128] + dts[:, b, :]
        out_field[:, :, 128 * b : 128 * b + 128] = value.reshape(LX, LY, 128).astype(BF16)
    wait_all(n_arrived)
    for d in range(PEERS):
        kgf[28 * d : 28 * d + 28] = r7[d]
    for group in range(14):
        turned = kgf[32 * group : 32 * group + 32].T
        for place in range(4):
            block = 4 * group + place
            if block < 54:
                out = out_k1 if block < 27 else out_k2
                out[block % 27] = turned[32 * place : 32 * place + 32]

    rim_done(xe, 0)
    rim_done(de, 1)
    for done in (
        x_done, y_done, m_done, c_done, x_done2, y_done2, m_done2, c_done2, k_done, l_done, n_done
    ):
        done()


def hand_over(*refs):
    for source, target in zip(refs[:4], refs[4:]):
        target[...] = source[...]


def shards(field, cotangent, kernel_one, kernel_two, spectral_weight):
    mz, mzs, tx, ty, tys = constants()
    vmem = pl.BlockSpec(memory_space=pltpu.VMEM)
    hbm = pl.BlockSpec(memory_space=pl.ANY)
    smem = pl.BlockSpec(memory_space=pltpu.SMEM)

    def buf(shape, dtype=F32):
        return pltpu.VMEM(shape, dtype)

    results = pl.pallas_call(
        body,
        out_shape=(
            jax.ShapeDtypeStruct((LX, LY, NZ * C), BF16),
            jax.ShapeDtypeStruct((27, C, C), F32),
            jax.ShapeDtypeStruct((27, C, C), F32),
            jax.ShapeDtypeStruct(spectral_weight.shape, F32),
        ),
        in_specs=[vmem, vmem, vmem, vmem, hbm, hbm, hbm, smem, vmem, vmem],
        out_specs=(vmem, vmem, vmem, vmem),
        scratch_shapes=[
            buf(spectral_weight.shape),
            buf(mz.shape, BF16),
            buf(mzs.shape, BF16),
            buf((256, 128)),
            buf((480, 128)),
            buf((8, 6, 16, 128), BF16),
            buf((8, 6, 16, 128), BF16),
            buf((2, 8, 6, 16, 256), BF16),
            buf((2, 6, 5, 16, 256), BF16),
            buf((2, 8, 6, 16, 256), BF16),
            buf((2, 6, 5, 16, 256), BF16),
            buf((480, 128)),
            buf((256, 128)),
            buf((4, 9, 256, 128), BF16),
            buf((32, 8, 128)),
            buf((2, LX, LY, 256)),
            buf((32, 8, 128)),
            buf((32, 8, 128)),
            buf((32, 1024), BF16),
            buf((2, 48, 16, 128), BF16),
            buf((2, 48, 16, 128), BF16),
            buf((2, PEERS, 9, 128)),
            buf((2, PEERS, 9, 128)),
            buf((128, 128)),
            buf((128, 128)),
            buf((144, 128)),
            buf((12, 16, 128)),
            buf((2, 1, 9, 128)),
            buf((2, PEERS, 9, 128)),
            buf((2, 3, 16, 128), BF16),
            buf((2, 48, 16, 128), BF16),
            buf((480, 128)),
            buf((PEERS, 32, 128), BF16),
            buf((PEERS, 32, 128), BF16),
            buf((1, 28, 128)),
            buf((PEERS, 28, 128)),
            buf((1, 28, 128)),
            buf((PEERS, 28, 128)),
            pltpu.SemaphoreType.DMA((2, 8)),
            pltpu.SemaphoreType.DMA((2, 8)),
            pltpu.SemaphoreType.DMA((6, PEERS)),
            pltpu.SemaphoreType.DMA((6, PEERS)),
            pltpu.SemaphoreType.DMA((5, PEERS)),
            pltpu.SemaphoreType.DMA((5, PEERS)),
            pltpu.SemaphoreType.DMA((3,)),
        ],
        compiler_params=pltpu.CompilerParams(
            collective_id=0, has_side_effects=True, vmem_limit_bytes=56 << 20
        ),
    )(field, cotangent, kernel_one, kernel_two, spectral_weight, mz, mzs, tx, ty, tys)
    return pl.pallas_call(
        hand_over,
        out_shape=tuple(jax.ShapeDtypeStruct(r.shape, r.dtype) for r in results),
        in_specs=[vmem] * 4,
        out_specs=(vmem,) * 4,
    )(*results)


def solution(mesh):
    return jax.shard_map(
        shards,
        mesh=mesh,
        in_specs=(
            P("gx", "gy", None),
            P("gx", "gy", None),
            P(),
            P(),
            P(None, ("gx", "gy"), None, None),
        ),
        out_specs=(P("gx", "gy", None), P(), P(), P(None, ("gx", "gy"), None, None)),
        check_vma=False,
    )
```

```python
import math

import jax
import jax.numpy as jnp
import numpy as np
from jax import lax
from jax.experimental import pallas as pl
from jax.experimental.pallas import tpu as pltpu
from jax.sharding import PartitionSpec as P

C = 32
MX = 24
MY = 24
MZ = 8
NZ = 32
NX = 64
NY = 128
PEERS = 16
LX = 4
LY = 8
MESH = pl.DeviceIdType.MESH
F32 = jnp.float32
BF16 = jnp.bfloat16
HIGH = lax.Precision.HIGHEST


def kept(length, count):
    half = count // 2
    return np.concatenate([np.arange(half), length - half + np.arange(half)])


def angles(coords, freqs, length):
    return (coords[:, None] * freqs[None, :] % length) * (2.0 * math.pi / length)


def split(table):
    high = table.astype(BF16)
    low = (table - high.astype(np.float64)).astype(BF16)
    return np.stack([high, low])


def constants():
    az = angles(np.arange(NZ), np.arange(MZ), NZ).reshape(NZ, 2, 4)
    fz = np.stack([np.cos(az), -np.sin(az)], axis=2)
    fz = fz.reshape(NZ, 2 * MZ)
    mz = np.repeat(fz, C, axis=1)
    mzs = np.repeat(fz.T, C, axis=1)
    ax = angles(np.arange(NX), kept(NX, MX), NX)
    tx = np.stack([np.cos(ax), np.sin(ax)], axis=-1).reshape(PEERS, LX, MX, 2)
    tx = tx.transpose(0, 2, 1, 3).reshape(PEERS, MX * LX * 2)
    ay = angles(np.arange(NY), kept(NY, MY), NY).reshape(PEERS, LY, 12, 2)
    cy = np.zeros((PEERS, 2, 16, LY))
    sy = np.zeros((PEERS, 2, 16, LY))
    cy[:, :, :12] = np.cos(ay).transpose(0, 3, 2, 1)
    sy[:, :, :12] = np.sin(ay).transpose(0, 3, 2, 1)
    ty = np.concatenate([cy, sy], axis=3).reshape(PEERS, 32, 16)
    tys = np.stack([cy, sy], axis=1).transpose(0, 1, 2, 4, 3).reshape(PEERS, 32, 16)
    return (
        split(mz).astype(np.float32),
        split(mzs).astype(np.float32),
        tx.astype(np.float32),
        ty.astype(np.float32),
        tys.astype(np.float32),
    )


def gelu_parts(x):
    k = math.sqrt(2.0 / math.pi)
    t = jnp.tanh(k * (x + 0.044715 * (x * x * x)))
    cdf = 0.5 * (1.0 + t)
    slope = cdf + x * (0.5 * (1.0 - t * t)) * (k * (1.0 + (3.0 * 0.044715) * (x * x)))
    return x * cdf, slope


def dot(a, b, precision=None):
    return jnp.dot(a, b, preferred_element_type=F32, precision=precision)


def body(
    field, cot, k1_hbm, k2_hbm, sw_hbm, fz, fzs, tx, ty_hbm, tys_hbm,
    out_field, out_k1, out_k2, out_sg,
    k1, k2, ty, tys, sw, sg, mz, mzs, taps, wide,
    xe, de, xw, hw, dw, pw, pre, brn, band, cg, zt, sp, dts, dtl,
    s1, r1, s2, r2, xs, xt, dys, yf, yg, s3, r3, s4, r4, kgf, kgb, r5, s6, r6, s7, r7,
    hs, hr, sx, rx, sy, ry, ls,
):
    gx = lax.axis_index("gx")
    gy = lax.axis_index("gy")
    loads = [
        pltpu.make_async_copy(k1_hbm, k1, ls.at[0]),
        pltpu.make_async_copy(k2_hbm, k2, ls.at[1]),
        pltpu.make_async_copy(ty_hbm.at[gy], ty, ls.at[2]),
        pltpu.make_async_copy(tys_hbm.at[gy], tys, ls.at[3]),
        pltpu.make_async_copy(sw_hbm, sw, ls.at[4]),
    ]
    for load in loads:
        load.start()

    zl, px = gx // 4, lax.rem(gx, 4)
    py, zc = gy // 4, lax.rem(gy, 4)

    def around(i, k):
        return lax.rem(i + k + PEERS, PEERS)

    barrier = pltpu.get_barrier_semaphore()

    @pl.loop(1, PEERS)
    def _(k):
        pl.semaphore_signal(barrier, inc=1, device_id=(around(gx, k), gy), device_id_type=MESH)
        pl.semaphore_signal(barrier, inc=1, device_id=(gx, around(gy, k)), device_id_type=MESH)

    for i in (-1, 1):
        for j in (-1, 1):
            pl.semaphore_signal(
                barrier, inc=1, device_id=(around(gx, i), around(gy, j)), device_id_type=MESH
            )

    for i in range(1, 4):
        for j in range(1, 4):
            for where in (
                (zl * 4 + lax.rem(px + i, 4), lax.rem(py + j, 4) * 4 + zc),
                (lax.rem(zl + i, 4) * 4 + px, py * 4 + lax.rem(zc + j, 4)),
            ):
                pl.semaphore_signal(barrier, inc=1, device_id=where, device_id_type=MESH)

    sides = [(i, j) for i in (-1, 0, 1) for j in (-1, 0, 1) if (i, j) != (0, 0)]
    x_from = {-1: (2, 2), 0: (2, 4), 1: (4, 2)}
    x_to = {-1: (6, 2), 0: (2, 4), 1: (0, 2)}
    y_from = {-1: (1, 1), 0: (1, 4), 1: (4, 1)}
    y_to = {-1: (5, 1), 0: (1, 4), 1: (0, 1)}

    def rim_copy(ext, which, n, i, j):
        return pltpu.make_async_remote_copy(
            src_ref=ext.at[pl.ds(*x_from[i]), pl.ds(*y_from[j])],
            dst_ref=ext.at[pl.ds(*x_to[i]), pl.ds(*y_to[j])],
            send_sem=hs.at[which, n],
            recv_sem=hr.at[which, n],
            device_id=(around(gx, i), around(gy, j)),
            device_id_type=MESH,
        )

    def rim_send(ext, which):
        for n, (i, j) in enumerate(sides):
            rim_copy(ext, which, n, i, j).start()

    def rim_wait(ext, which):
        for n, (i, j) in enumerate(sides):
            rim_copy(ext, which, n, i, j).wait_recv()

    def rim_done(ext, which):
        for n, (i, j) in enumerate(sides):
            rim_copy(ext, which, n, i, j).wait_send()

    def exchange(axis, src, dst, which, scatter, n):
        me = {"gx": gx, "gy": gy, "xy": px * 4 + py, "z": zl * 4 + zc}[axis]
        send, recv = (sy, ry) if axis == "gy" else (sx, rx)

        def device(peer):
            if axis == "gx":
                return (peer, gy)
            if axis == "gy":
                return (gx, peer)
            if axis == "xy":
                return (zl * 4 + peer // 4, lax.rem(peer, 4) * 4 + zc)
            return (peer // 4 * 4 + px, py * 4 + lax.rem(peer, 4))

        def copy(k, peer, slot):
            return pltpu.make_async_remote_copy(
                src_ref=src.at[pl.ds(n * peer if scatter else 0, n)],
                dst_ref=dst.at[pl.ds(n * slot, n)],
                send_sem=send.at[which, k],
                recv_sem=recv.at[which, k],
                device_id=device(peer),
                device_id_type=MESH,
            )

        def start(k):
            copy(k, around(me, k), me).start()

        def arrived(k):
            peer = around(me, -k)
            copy(k, peer, peer).wait_recv()

        def done():
            @pl.loop(1, PEERS)
            def _(k):
                copy(k, around(me, k), me).wait_send()

        return start, arrived, done

    def start_all(start):
        @pl.loop(1, PEERS)
        def _(k):
            start(k)

    def wait_all(arrived):
        @pl.loop(1, PEERS)
        def _(k):
            arrived(k)

    def total_of(dst, n):
        def add(k, acc):
            return acc + dst[pl.ds(n * k, n)].astype(F32)

        return lax.fori_loop(0, PEERS, add, jnp.zeros((n,) + dst.shape[1:], F32))

    def spread(table, made, n, width):
        row = lax.broadcasted_iota(jnp.int32, (C, width), 0)
        unit = row == lax.rem(lax.broadcasted_iota(jnp.int32, (C, width), 1), C)
        for part in range(2):

            @pl.loop(0, n)
            def _(i):
                wide_row = jnp.broadcast_to(table[part, pl.ds(i, 1), :], (C, width))
                at = pl.ds(pl.multiple_of(i * C, C), C)
                made[part, at, :] = jnp.where(unit, wide_row, 0.0).astype(BF16)

    def z_modes(rows):
        modes = dot(rows, mz[0]) + dot(rows, mz[1])
        for h in range(2):
            zt[h] = modes[:, 256 * h : 256 * h + 256].reshape(LX, LY, 256)

    def x_send(which):
        start, arrived, done = exchange("gx", s1.at[which], r1.at[which], which, True, 3)

        def units(peer):
            for j in range(3):
                unit = 3 * peer + j
                ix = unit // 2
                half = lax.rem(unit, 2)
                re = jnp.zeros((LY, 128), F32)
                im = jnp.zeros((LY, 128), F32)
                for x in range(LX):
                    c = tx[gx, ix * 8 + 2 * x]
                    s = tx[gx, ix * 8 + 2 * x + 1]
                    zr = zt[half, x, :, 0:128]
                    zi = zt[half, x, :, 128:256]
                    re = re + (c * zr + s * zi)
                    im = im + (c * zi - s * zr)
                s1[which, unit] = jnp.concatenate([re, im], axis=0).astype(BF16)

        @pl.loop(1, PEERS)
        def _(k):
            units(around(gx, k))
            start(k)

        units(gx)
        r1[which, pl.ds(3 * gx, 3)] = s1[which, pl.ds(3 * gx, 3)]
        return arrived, done

    lane = lax.broadcasted_iota(jnp.int32, (LY, 128), 1)

    def y_send(which):
        part = total_of(r1.at[which], 3)
        blocks = []
        for u in range(3):
            re = part[u, 0:8]
            im = part[u, 8:16]
            for k in range(4):
                here = (128 - 32 * k) % 128
                after = (160 - 32 * k) % 128
                re_here = pltpu.roll(re, here, 1) if here else re
                im_here = pltpu.roll(im, here, 1) if here else im
                re_after = pltpu.roll(re, after, 1) if after else re
                im_after = pltpu.roll(im, after, 1) if after else im
                straight = jnp.where(lane < 32, re_here, jnp.where(lane < 64, im_after, 0.0))
                crossed = jnp.where(lane < 32, im_here, jnp.where(lane < 64, -re_after, 0.0))
                blocks.append(jnp.concatenate([straight, crossed], axis=0))
        modes = dot(ty[...], jnp.concatenate(blocks, axis=1), HIGH)
        for p in range(12):
            at = 128 * p
            rows = modes[0:16, at : at + 128] + pltpu.roll(modes[16:32, at : at + 128], 64, 1)
            yf[12 * p : 12 * p + 12] = rows[0:12]
        for d in range(PEERS):
            s2[which, d] = yf[9 * d : 9 * d + 9]
        start, arrived, done = exchange("gy", s2.at[which], r2.at[which], 2 * which, True, 1)
        start_all(start)
        r2[which, gy] = s2[which, gy]
        return arrived, done

    def modes_send(which):
        start, arrived, done = exchange("gy", s3.at[which], r3.at[which], 2 * which + 1, False, 1)
        start_all(start)
        r3[which, gy] = s3[which, 0]
        return arrived, done

    def columns_send(which):
        for d in range(PEERS):
            row = 9 * d
            while row < 9 * d + 9:
                p = row // 12
                end = min(9 * d + 9, 12 * p + 12)
                yg[p, row - 12 * p : end - 12 * p] = r3[which, d, row - 9 * d : end - 9 * d]
                row = end
        cells = dot(tys[...], jnp.concatenate([yg[p] for p in range(12)], axis=1), HIGH)
        for u in range(3):
            re = jnp.zeros((LY, 128), F32)
            im = jnp.zeros((LY, 128), F32)
            for k in range(4):
                at = 128 * (4 * u + k)
                cell = cells[:, at : at + 128]
                cosine = cell[0:8] + pltpu.roll(cell[8:16], 64, 1)
                sine = cell[16:24] + pltpu.roll(cell[24:32], 64, 1)
                both = cosine + jnp.where(
                    lane < 32, -pltpu.roll(sine, 96, 1), pltpu.roll(sine, 32, 1)
                )
                mine = lane // 32 == k
                up = 32 * k
                down = (32 * k + 96) % 128
                re = jnp.where(mine, pltpu.roll(both, up, 1) if up else both, re)
                im = jnp.where(mine, pltpu.roll(both, down, 1) if down else both, im)
            s4[which, u] = jnp.concatenate([re, im], axis=0).astype(BF16)
        start, arrived, done = exchange("gx", s4.at[which], r4.at[which], 2 + which, False, 3)
        start_all(start)
        r4[which, pl.ds(3 * gx, 3)] = s4[which]
        return arrived, done

    def cells_of(which):
        def step(jj, acc):
            acc = list(acc)
            for t in range(3):
                ix = 3 * jj + t
                for h in range(2):
                    unit = r4[which, 6 * jj + 2 * t + h].astype(F32)
                    re = unit[0:8]
                    im = unit[8:16]
                    for x in range(LX):
                        c = tx[gx, ix * 8 + 2 * x]
                        s = tx[gx, ix * 8 + 2 * x + 1]
                        at = (h * LX + x) * 2
                        acc[at] = acc[at] + (c * re - s * im)
                        acc[at + 1] = acc[at + 1] + (c * im + s * re)
            return tuple(acc)

        zero = jnp.zeros((LY, 128), F32)
        acc = lax.fori_loop(0, 8, step, (zero,) * 16)
        rows = [
            jnp.concatenate([acc[x * 2], acc[x * 2 + 1], acc[8 + x * 2], acc[9 + x * 2]], axis=1)
            for x in range(LX)
        ]
        modes = jnp.concatenate(rows, axis=0)
        high = modes.astype(BF16)
        low = (modes - high.astype(F32)).astype(BF16)
        return dot(high, mzs[0]) + (dot(high, mzs[1]) + dot(low, mzs[0]))

    def windows(dst, i, values):
        n = values.shape[0]
        zb = lax.broadcasted_iota(jnp.int32, (n, 8, 128), 1)
        ln = lax.broadcasted_iota(jnp.int32, (n, 8, 128), 2)
        before = pltpu.roll(values, 1, 1)
        after = pltpu.roll(values, 7, 1)
        edge = jnp.where(
            (ln >= 96) & (zb > 0), before, jnp.where((ln < 32) & (zb < 7), after, 0.0)
        )
        for part, lanes in ((values, 0), (edge, 128)):
            even = part.reshape(n // 2, 16, 128).astype(BF16)
            odd = part[1 : n - 1].reshape(n // 2 - 1, 16, 128).astype(BF16)
            dst[0, i, :, :, lanes : lanes + 128] = even
            dst[1, i, 0 : n // 2 - 1, :, lanes : lanes + 128] = odd

    def conv(src, kernel, nx, ny, acc):
        total = jnp.zeros((nx * ny * 8, 128), F32)
        for ab in range(9):
            a, b = divmod(ab, 3)
            rows = src[b % 2, a : a + nx, b // 2 : b // 2 + ny // 2].reshape(nx * ny * 8, 256)
            total = total + dot(rows, band[kernel, ab])
        acc[...] = total

    def correlate(src, off, grad, q):
        turned = grad.T.astype(BF16)

        lanes = lax.broadcasted_iota(jnp.int32, (C, 256), 1)
        for ab in range(9):
            a, b = divmod(ab, 3)
            a, b = a + off, b + off
            rows = src[b % 2, a : a + LX, b // 2 : b // 2 + LY // 2].reshape(256, 256)
            prod = dot(turned, rows)
            group, place = divmod(ab * 3, 4)
            first_lane = 32 * place
            acc = jnp.zeros((C, 256), F32)
            for zl in range(4):
                shift = (32 - 32 * zl + first_lane) % 256
                piece = prod[32 * zl : 32 * zl + 32]
                acc = acc + (pltpu.roll(piece, shift, 1) if shift else piece)
            acc = jnp.where((lanes >= first_lane) & (lanes < first_lane + 96), acc, 0.0)
            kgf[q, 32 * group : 32 * group + 32] += acc[:, 0:128]
            if first_lane + 96 > 128:
                kgf[q, 32 * group + 32 : 32 * group + 64] += acc[:, 128:256]
        for d in range(PEERS):
            kgb[q, d] = kgf[q, 14 * d : 14 * d + 16].astype(BF16)

    def grad_scatter(q):
        start, arrived, done = exchange("xy", kgb.at[q], r5.at[q], 4 + q, True, 1)
        start_all(start)
        r5[q, px * 4 + py] = kgb[q, px * 4 + py]
        return arrived, done

    def grad_sum(q):
        s6[q, 0] = total_of(r5.at[q], 1)[0, 0:14]
        start, arrived, done = exchange("z", s6.at[q], r6.at[q], 8 + q, False, 1)
        start_all(start)
        r6[q, zl * 4 + zc] = s6[q, 0]
        return arrived, done

    def grad_gather(q):
        s7[q] = total_of(r6.at[q], 1)
        start, arrived, done = exchange("xy", s7.at[q], r7.at[q], 6 + q, False, 1)
        start_all(start)
        r7[q, px * 4 + py] = s7[q, 0]
        return arrived, done

    def widen(ext, dst):
        @pl.loop(0, 8)
        def _(i):
            values = ext[i].astype(F32).reshape(12, 8, 128)
            yi = lax.broadcasted_iota(jnp.int32, (12, 8, 128), 0) + (gy * LY - 2)
            row = gx * LX - 2 + i
            ok = (row >= 0) & (row < NX) & (yi >= 0) & (yi < NY)
            windows(dst, i, jnp.where(ok, values, 0.0))

    for x in range(LX):
        mine = field[x].astype(F32)
        g = cot[x].astype(F32)
        for b in range(8):
            sp[8 * x : 8 * x + 8, b, :] = mine[:, 128 * b : 128 * b + 128]
            cg[8 * x : 8 * x + 8, b, :] = g[:, 128 * b : 128 * b + 128]
    xe[2:6, 1:5] = sp[...].reshape(4, 4, 16, 128).astype(BF16)
    spread(fz, mz, NZ, 2 * MZ * C)
    z_modes(field[...].reshape(32, 1024))

    pl.semaphore_wait(barrier, 2 * (PEERS - 1) + 22)

    x_arrived, x_done = x_send(0)

    for load in loads[:4]:
        load.wait()
    group = lax.broadcasted_iota(jnp.int32, (C, 128), 1) // C
    for q, kernel in ((0, k1), (1, k2)):

        @pl.loop(0, 9)
        def _(ab):
            wide = []
            for e in range(3):
                tap = kernel[3 * ab + e].astype(F32)
                wide.append(jnp.concatenate([tap] * 4, axis=1))
            for block in range(8):
                z = block if block < 5 else block - 8
                rows = jnp.zeros((C, 128), F32)
                for e in range(3):
                    if 0 <= z + 1 - e < 4:
                        rows = jnp.where(group == z + 1 - e, wide[e], rows)
                taps[32 * block : 32 * block + 32] = rows
            band[q, ab] = taps[...].astype(BF16)
            band[3 - q, 8 - ab, 0:128] = taps[0:128].T.astype(BF16)
            band[3 - q, 8 - ab, 128:256] = taps[128:256].T.astype(BF16)

    kgf[...] = jnp.zeros_like(kgf)
    yg[...] = jnp.zeros_like(yg)


    wait_all(x_arrived)
    y_arrived, y_done = y_send(0)

    rim_send(xe, 0)
    spread(fzs, mzs, 2 * MZ, NZ * C)

    wait_all(y_arrived)
    loads[4].wait()
    first = (gx * PEERS + gy) * 18

    def scale_of(m):
        kz = lax.rem((first + m) // MY, MZ)
        return jnp.where(kz == 0, 1.0 / (NX * NY * NZ), 2.0 / (NX * NY * NZ)).astype(F32)

    xs[...] = jnp.zeros_like(xs)
    xs[0:9] = total_of(r2.at[0], 1)[0]
    xt[...] = xs[...].T
    for t in range(9):
        row = []
        for half in range(2):
            m = 2 * t + half
            xr = xt[64 * half : 64 * half + 32, t : t + 1]
            xi = xt[64 * half + 32 : 64 * half + 64, t : t + 1]
            wr = sw[0, m]
            wi = sw[1, m]
            row.append(jnp.sum(xr * wr - xi * wi, axis=0, keepdims=True) * scale_of(m))
            row.append(jnp.sum(xr * wi + xi * wr, axis=0, keepdims=True) * scale_of(m))
        s3[0, 0, t : t + 1, :] = jnp.concatenate(row, axis=1)
    m_arrived, m_done = modes_send(0)

    rim_wait(xe, 0)
    widen(xe, xw)
    conv(xw, 0, 6, 10, pre)

    wait_all(m_arrived)
    c_arrived, c_done = columns_send(0)

    @pl.loop(0, 6)
    def _(i):
        rows = pl.ds(pl.multiple_of(i * 80, 80), 80)
        h, slope = gelu_parts(pre[rows])
        pre[rows] = slope
        yi = lax.broadcasted_iota(jnp.int32, (10, 8, 128), 0) + (gy * LY - 1)
        row = gx * LX - 1 + i
        ok = (row >= 0) & (row < NX) & (yi >= 0) & (yi < NY)
        h = h.astype(BF16).astype(F32).reshape(10, 8, 128)
        windows(hw, i, jnp.where(ok, h, 0.0))

    conv(hw, 1, 4, 8, brn)

    wait_all(c_arrived)
    spectral = cells_of(0)
    for b in range(8):
        sp[:, b, :] = spectral[:, 128 * b : 128 * b + 128]

    _, slope = gelu_parts(sp[...].reshape(256, 128) + brn[...])
    dtotal = (cg[...].reshape(256, 128) * slope).astype(BF16)
    de[2:6, 1:5] = dtotal.reshape(4, 4, 16, 128)
    rim_send(de, 1)
    dts[...] = dtotal.astype(F32).reshape(32, 8, 128)
    for b in range(8):
        dtl[:, 128 * b : 128 * b + 128] = dts[:, b, :].astype(BF16)
    z_modes(dtl[...])
    x_arrived2, x_done2 = x_send(1)

    correlate(hw, 0, dts[...].reshape(256, 128), 1)
    k_arrived2, k_done2 = grad_scatter(1)
    rim_wait(de, 1)
    widen(de, dw)
    conv(dw, 2, 6, 10, wide)

    @pl.loop(0, 6)
    def _(i):
        rows = pl.ds(pl.multiple_of(i * 80, 80), 80)
        dpre = (wide[rows] * pre[rows]).astype(BF16).astype(F32).reshape(10, 8, 128)
        yi = lax.broadcasted_iota(jnp.int32, (10, 8, 128), 0) + (gy * LY - 1)
        row = gx * LX - 1 + i
        ok = (row >= 0) & (row < NX) & (yi >= 0) & (yi < NY)
        windows(pw, i, jnp.where(ok, dpre, 0.0))

    own = pw[1, 1:5, 0:4, :, 0:128].reshape(256, 128).astype(F32)
    correlate(xw, 1, own, 0)
    k_arrived, k_done = grad_scatter(0)

    wait_all(x_arrived2)
    y_arrived2, y_done2 = y_send(1)
    wait_all(k_arrived2)
    l_arrived2, l_done2 = grad_sum(1)
    conv(pw, 3, 4, 8, brn)

    wait_all(y_arrived2)
    xs[0:9] = total_of(r2.at[1], 1)[0]
    mode_lane = lax.broadcasted_iota(jnp.int32, (128, 128), 1)
    back = jnp.zeros((128, 128), F32)
    for t in range(9):
        column = []
        dy = xs[t : t + 1, :] * scale_of(2 * t)
        dys[t : t + 1, :] = dy
        for half in range(2):
            m = 2 * t + half
            wr = sw[0, m]
            wi = sw[1, m]
            dyr = dy[:, 64 * half : 64 * half + 32]
            dyi = dy[:, 64 * half + 32 : 64 * half + 64]
            column.append(jnp.sum(wr * dyr + wi * dyi, axis=1, keepdims=True))
            column.append(jnp.sum(wr * dyi - wi * dyr, axis=1, keepdims=True))
        back = jnp.where(mode_lane == t, jnp.concatenate(column, axis=0), back)
    xs[...] = back.T
    s3[1, 0] = xs[0:9]
    m_arrived2, m_done2 = modes_send(1)
    for t in range(9):
        for half in range(2):
            m = 2 * t + half
            xr = xt[64 * half : 64 * half + 32, t : t + 1]
            xi = xt[64 * half + 32 : 64 * half + 64, t : t + 1]
            dyr = dys[t : t + 1, 64 * half : 64 * half + 32]
            dyi = dys[t : t + 1, 64 * half + 32 : 64 * half + 64]
            sg[0, m] = xr * dyr + xi * dyi
            sg[1, m] = xr * dyi - xi * dyr
    save = pltpu.make_async_copy(sg, out_sg, ls.at[5])
    save.start()

    wait_all(k_arrived)
    l_arrived, l_done = grad_sum(0)
    wait_all(m_arrived2)
    c_arrived2, c_done2 = columns_send(1)

    wait_all(l_arrived2)
    n_arrived2, n_done2 = grad_gather(1)
    wait_all(l_arrived)
    n_arrived, n_done = grad_gather(0)

    wait_all(c_arrived2)
    spectral = cells_of(1)
    dts[...] = brn[...].reshape(32, 8, 128)
    for b in range(8):
        value = spectral[:, 128 * b : 128 * b + 128] + dts[:, b, :]
        out_field[:, :, 128 * b : 128 * b + 128] = value.reshape(LX, LY, 128).astype(BF16)
    for q, waiting, out in ((1, n_arrived2, out_k2), (0, n_arrived, out_k1)):
        wait_all(waiting)
        for d in range(PEERS):
            kgf[q, 14 * d : 14 * d + 14] = r7[q, d]
        for group in range(7):
            turned = kgf[q, 32 * group : 32 * group + 32].T
            for place in range(min(4, 27 - 4 * group)):
                out[4 * group + place] = turned[32 * place : 32 * place + 32]

    save.wait()
    rim_done(xe, 0)
    rim_done(de, 1)
    for done in (
        x_done, y_done, m_done, c_done, x_done2, y_done2, m_done2, c_done2, k_done, l_done, n_done,
        k_done2, l_done2, n_done2,
    ):
        done()


def hand_over(*refs):
    results, outs, kept_here = refs[0:4], refs[4:8], refs[8:12]
    into, out = refs[12:14]
    loads = [pltpu.make_async_copy(results[i], kept_here[i], into.at[i]) for i in range(4)]
    saves = [pltpu.make_async_copy(kept_here[i], outs[i], out.at[i]) for i in range(4)]
    for load in loads:
        load.start()
    for load, save in zip(loads, saves):
        load.wait()
        save.start()
    for save in saves:
        save.wait()


def shards(field, cotangent, kernel_one, kernel_two, spectral_weight):
    mz, mzs, tx, ty, tys = constants()
    vmem = pl.BlockSpec(memory_space=pltpu.VMEM)
    hbm = pl.BlockSpec(memory_space=pl.ANY)
    smem = pl.BlockSpec(memory_space=pltpu.SMEM)

    def buf(shape, dtype=F32):
        return pltpu.VMEM(shape, dtype)

    results = pl.pallas_call(
        body,
        out_shape=(
            jax.ShapeDtypeStruct((LX, LY, NZ * C), BF16),
            jax.ShapeDtypeStruct((27, C, C), F32),
            jax.ShapeDtypeStruct((27, C, C), F32),
            jax.ShapeDtypeStruct(spectral_weight.shape, F32),
        ),
        in_specs=[vmem, vmem, hbm, hbm, hbm, vmem, vmem, smem, hbm, hbm],
        out_specs=(vmem, vmem, vmem, hbm),
        scratch_shapes=[
            buf((27, C, C), BF16),
            buf((27, C, C), BF16),
            buf((32, 16)),
            buf((32, 16)),
            buf(spectral_weight.shape),
            buf(spectral_weight.shape),
            buf((2, NZ * C, 2 * MZ * C), BF16),
            buf((2, 2 * MZ * C, NZ * C), BF16),
            buf((256, 128)),
            buf((480, 128)),
            buf((8, 6, 16, 128), BF16),
            buf((8, 6, 16, 128), BF16),
            buf((2, 8, 6, 16, 256), BF16),
            buf((2, 6, 5, 16, 256), BF16),
            buf((2, 8, 6, 16, 256), BF16),
            buf((2, 6, 5, 16, 256), BF16),
            buf((480, 128)),
            buf((256, 128)),
            buf((4, 9, 256, 128), BF16),
            buf((32, 8, 128)),
            buf((2, LX, LY, 256)),
            buf((32, 8, 128)),
            buf((32, 8, 128)),
            buf((32, 1024), BF16),
            buf((2, 48, 16, 128), BF16),
            buf((2, 48, 16, 128), BF16),
            buf((2, PEERS, 9, 128)),
            buf((2, PEERS, 9, 128)),
            buf((128, 128)),
            buf((128, 128)),
            buf((16, 128)),
            buf((144, 128)),
            buf((12, 16, 128)),
            buf((2, 1, 9, 128)),
            buf((2, PEERS, 9, 128)),
            buf((2, 3, 16, 128), BF16),
            buf((2, 48, 16, 128), BF16),
            buf((2, 256, 128)),
            buf((2, PEERS, 16, 128), BF16),
            buf((2, PEERS, 16, 128), BF16),
            buf((2, 1, 14, 128)),
            buf((2, PEERS, 14, 128)),
            buf((2, 1, 14, 128)),
            buf((2, PEERS, 14, 128)),
            pltpu.SemaphoreType.DMA((2, 8)),
            pltpu.SemaphoreType.DMA((2, 8)),
            pltpu.SemaphoreType.DMA((10, PEERS)),
            pltpu.SemaphoreType.DMA((10, PEERS)),
            pltpu.SemaphoreType.DMA((4, PEERS)),
            pltpu.SemaphoreType.DMA((4, PEERS)),
            pltpu.SemaphoreType.DMA((6,)),
        ],
        compiler_params=pltpu.CompilerParams(
            collective_id=0, has_side_effects=True, vmem_limit_bytes=56 << 20
        ),
    )(field, cotangent, kernel_one, kernel_two, spectral_weight, mz, mzs, tx, ty, tys)
    return pl.pallas_call(
        hand_over,
        out_shape=tuple(jax.ShapeDtypeStruct(r.shape, r.dtype) for r in results),
        in_specs=[hbm] * 4,
        out_specs=(hbm,) * 4,
        scratch_shapes=[buf(r.shape, r.dtype) for r in results]
        + [pltpu.SemaphoreType.DMA((4,)), pltpu.SemaphoreType.DMA((4,))],
    )(*results)


def solution(mesh):
    return jax.shard_map(
        shards,
        mesh=mesh,
        in_specs=(
            P("gx", "gy", None),
            P("gx", "gy", None),
            P(),
            P(),
            P(None, ("gx", "gy"), None, None),
        ),
        out_specs=(P("gx", "gy", None), P(), P(), P(None, ("gx", "gy"), None, None)),
        check_vma=False,
    )
```

```python
import math

import jax
import jax.numpy as jnp
import numpy as np
from jax import lax
from jax.experimental import pallas as pl
from jax.experimental.pallas import tpu as pltpu
from jax.sharding import PartitionSpec as P

C = 32
MX = 24
MY = 24
MZ = 8
NZ = 32
NX = 64
NY = 128
PEERS = 16
LX = 4
LY = 8
MESH = pl.DeviceIdType.MESH
F32 = jnp.float32
BF16 = jnp.bfloat16
HIGH = lax.Precision.HIGHEST


def kept(length, count):
    half = count // 2
    return np.concatenate([np.arange(half), length - half + np.arange(half)])


def angles(coords, freqs, length):
    return (coords[:, None] * freqs[None, :] % length) * (2.0 * math.pi / length)


def split(table):
    high = table.astype(BF16)
    low = (table - high.astype(np.float64)).astype(BF16)
    return np.stack([high, low])


def constants():
    az = angles(np.arange(NZ), np.arange(MZ), NZ).reshape(NZ, 2, 4)
    fz = np.stack([np.cos(az), -np.sin(az)], axis=2)
    fz = fz.reshape(NZ, 2 * MZ)
    mz = np.repeat(fz, C, axis=1)
    mzs = np.repeat(fz.T, C, axis=1)
    ax = angles(np.arange(NX), kept(NX, MX), NX)
    tx = np.stack([np.cos(ax), np.sin(ax)], axis=-1).reshape(PEERS, LX, MX, 2)
    tx = tx.transpose(0, 2, 1, 3).reshape(PEERS, MX * LX * 2)
    ay = angles(np.arange(NY), kept(NY, MY), NY).reshape(PEERS, LY, 12, 2)
    cy = np.zeros((PEERS, 2, 16, LY))
    sy = np.zeros((PEERS, 2, 16, LY))
    cy[:, :, :12] = np.cos(ay).transpose(0, 3, 2, 1)
    sy[:, :, :12] = np.sin(ay).transpose(0, 3, 2, 1)
    ty = np.concatenate([cy, sy], axis=3).reshape(PEERS, 32, 16)
    tys = np.stack([cy, sy], axis=1).transpose(0, 1, 2, 4, 3).reshape(PEERS, 32, 16)
    return (
        split(mz).astype(np.float32),
        split(mzs).astype(np.float32),
        tx.astype(np.float32),
        ty.astype(np.float32),
        tys.astype(np.float32),
    )


def gelu_parts(x):
    k = math.sqrt(2.0 / math.pi)
    t = jnp.tanh(k * (x + 0.044715 * (x * x * x)))
    cdf = 0.5 * (1.0 + t)
    slope = cdf + x * (0.5 * (1.0 - t * t)) * (k * (1.0 + (3.0 * 0.044715) * (x * x)))
    return x * cdf, slope


def dot(a, b, precision=None):
    return jnp.dot(a, b, preferred_element_type=F32, precision=precision)


def body(
    field, cot, k1_hbm, k2_hbm, sw_hbm, fz, fzs, tx, ty_hbm, tys_hbm,
    out_field, out_k1, out_k2, out_sg,
    k1, k2, ty, tys, sw, sg, mz, mzs, taps, wide,
    xe, de, xw, hw, dw, pw, pre, brn, band, cg, zt, sp, dts, dtl,
    s1, r1, s2, r2, xs, xt, dys, yf, yg, s3, r3, s4, r4, kgf, kgb, r5, s6, r6, s7, r7,
    hs, hr, sx, rx, sy, ry, ls,
):
    gx = lax.axis_index("gx")
    gy = lax.axis_index("gy")
    loads = [
        pltpu.make_async_copy(k1_hbm, k1, ls.at[0]),
        pltpu.make_async_copy(k2_hbm, k2, ls.at[1]),
        pltpu.make_async_copy(ty_hbm.at[gy], ty, ls.at[2]),
        pltpu.make_async_copy(tys_hbm.at[gy], tys, ls.at[3]),
        pltpu.make_async_copy(sw_hbm, sw, ls.at[4]),
    ]
    for load in loads:
        load.start()

    zl, px = gx // 4, lax.rem(gx, 4)
    py, zc = gy // 4, lax.rem(gy, 4)

    def around(i, k):
        return lax.rem(i + k + PEERS, PEERS)

    barrier = pltpu.get_barrier_semaphore()

    @pl.loop(1, PEERS)
    def _(k):
        pl.semaphore_signal(barrier, inc=1, device_id=(around(gx, k), gy), device_id_type=MESH)
        pl.semaphore_signal(barrier, inc=1, device_id=(gx, around(gy, k)), device_id_type=MESH)

    for i in (-1, 1):
        for j in (-1, 1):
            pl.semaphore_signal(
                barrier, inc=1, device_id=(around(gx, i), around(gy, j)), device_id_type=MESH
            )

    for i in range(1, 4):
        for j in range(1, 4):
            for where in (
                (zl * 4 + lax.rem(px + i, 4), lax.rem(py + j, 4) * 4 + zc),
                (lax.rem(zl + i, 4) * 4 + px, py * 4 + lax.rem(zc + j, 4)),
            ):
                pl.semaphore_signal(barrier, inc=1, device_id=where, device_id_type=MESH)

    sides = [(i, j) for i in (-1, 0, 1) for j in (-1, 0, 1) if (i, j) != (0, 0)]
    x_from = {-1: (2, 2), 0: (2, 4), 1: (4, 2)}
    x_to = {-1: (6, 2), 0: (2, 4), 1: (0, 2)}
    y_from = {-1: (1, 1), 0: (1, 4), 1: (4, 1)}
    y_to = {-1: (5, 1), 0: (1, 4), 1: (0, 1)}

    def rim_copy(ext, which, n, i, j):
        return pltpu.make_async_remote_copy(
            src_ref=ext.at[pl.ds(*x_from[i]), pl.ds(*y_from[j])],
            dst_ref=ext.at[pl.ds(*x_to[i]), pl.ds(*y_to[j])],
            send_sem=hs.at[which, n],
            recv_sem=hr.at[which, n],
            device_id=(around(gx, i), around(gy, j)),
            device_id_type=MESH,
        )

    def rim_send(ext, which):
        for n, (i, j) in enumerate(sides):
            rim_copy(ext, which, n, i, j).start()

    def rim_wait(ext, which):
        for n, (i, j) in enumerate(sides):
            rim_copy(ext, which, n, i, j).wait_recv()

    def rim_done(ext, which):
        for n, (i, j) in enumerate(sides):
            rim_copy(ext, which, n, i, j).wait_send()

    def exchange(axis, src, dst, which, scatter, n):
        me = {"gx": gx, "gy": gy, "xy": px * 4 + py, "z": zl * 4 + zc}[axis]
        send, recv = (sy, ry) if axis == "gy" else (sx, rx)

        def device(peer):
            if axis == "gx":
                return (peer, gy)
            if axis == "gy":
                return (gx, peer)
            if axis == "xy":
                return (zl * 4 + peer // 4, lax.rem(peer, 4) * 4 + zc)
            return (peer // 4 * 4 + px, py * 4 + lax.rem(peer, 4))

        def copy(k, peer, slot):
            return pltpu.make_async_remote_copy(
                src_ref=src.at[pl.ds(n * peer if scatter else 0, n)],
                dst_ref=dst.at[pl.ds(n * slot, n)],
                send_sem=send.at[which, k],
                recv_sem=recv.at[which, k],
                device_id=device(peer),
                device_id_type=MESH,
            )

        def start(k):
            copy(k, around(me, k), me).start()

        def arrived(k):
            peer = around(me, -k)
            copy(k, peer, peer).wait_recv()

        def done():
            @pl.loop(1, PEERS)
            def _(k):
                copy(k, around(me, k), me).wait_send()

        return start, arrived, done

    def start_all(start):
        @pl.loop(1, PEERS)
        def _(k):
            start(k)

    def wait_all(arrived):
        @pl.loop(1, PEERS)
        def _(k):
            arrived(k)

    def total_of(dst, n):
        def add(k, acc):
            return acc + dst[pl.ds(n * k, n)].astype(F32)

        return lax.fori_loop(0, PEERS, add, jnp.zeros((n,) + dst.shape[1:], F32))

    def spread(table, made, n, width):
        row = lax.broadcasted_iota(jnp.int32, (C, width), 0)
        unit = row == lax.rem(lax.broadcasted_iota(jnp.int32, (C, width), 1), C)
        for part in range(2):

            @pl.loop(0, n)
            def _(i):
                wide_row = jnp.broadcast_to(table[part, pl.ds(i, 1), :], (C, width))
                at = pl.ds(pl.multiple_of(i * C, C), C)
                made[part, at, :] = jnp.where(unit, wide_row, 0.0).astype(BF16)

    def z_modes(rows):
        modes = dot(rows, mz[0]) + dot(rows, mz[1])
        for h in range(2):
            zt[h] = modes[:, 256 * h : 256 * h + 256].reshape(LX, LY, 256)

    def x_send(which):
        start, arrived, done = exchange("gx", s1.at[which], r1.at[which], which, True, 3)

        def units(peer):
            for j in range(3):
                unit = 3 * peer + j
                ix = unit // 2
                half = lax.rem(unit, 2)
                re = jnp.zeros((LY, 128), F32)
                im = jnp.zeros((LY, 128), F32)
                for x in range(LX):
                    c = tx[gx, ix * 8 + 2 * x]
                    s = tx[gx, ix * 8 + 2 * x + 1]
                    zr = zt[half, x, :, 0:128]
                    zi = zt[half, x, :, 128:256]
                    re = re + (c * zr + s * zi)
                    im = im + (c * zi - s * zr)
                s1[which, unit] = jnp.concatenate([re, im], axis=0).astype(BF16)

        @pl.loop(1, PEERS)
        def _(k):
            units(around(gx, k))
            start(k)

        units(gx)
        r1[which, pl.ds(3 * gx, 3)] = s1[which, pl.ds(3 * gx, 3)]
        return arrived, done

    lane = lax.broadcasted_iota(jnp.int32, (LY, 128), 1)

    def y_send(which):
        part = total_of(r1.at[which], 3)
        blocks = []
        for u in range(3):
            re = part[u, 0:8]
            im = part[u, 8:16]
            for k in range(4):
                here = (128 - 32 * k) % 128
                after = (160 - 32 * k) % 128
                re_here = pltpu.roll(re, here, 1) if here else re
                im_here = pltpu.roll(im, here, 1) if here else im
                re_after = pltpu.roll(re, after, 1) if after else re
                im_after = pltpu.roll(im, after, 1) if after else im
                straight = jnp.where(lane < 32, re_here, jnp.where(lane < 64, im_after, 0.0))
                crossed = jnp.where(lane < 32, im_here, jnp.where(lane < 64, -re_after, 0.0))
                blocks.append(jnp.concatenate([straight, crossed], axis=0))
        modes = dot(ty[...], jnp.concatenate(blocks, axis=1), HIGH)
        for p in range(12):
            at = 128 * p
            rows = modes[0:16, at : at + 128] + pltpu.roll(modes[16:32, at : at + 128], 64, 1)
            yf[12 * p : 12 * p + 12] = rows[0:12]
        for d in range(PEERS):
            s2[which, d] = yf[9 * d : 9 * d + 9]
        start, arrived, done = exchange("gy", s2.at[which], r2.at[which], 2 * which, True, 1)
        start_all(start)
        r2[which, gy] = s2[which, gy]
        return arrived, done

    def modes_send(which):
        start, arrived, done = exchange("gy", s3.at[which], r3.at[which], 2 * which + 1, False, 1)
        start_all(start)
        r3[which, gy] = s3[which, 0]
        return arrived, done

    def columns_send(which):
        for d in range(PEERS):
            row = 9 * d
            while row < 9 * d + 9:
                p = row // 12
                end = min(9 * d + 9, 12 * p + 12)
                yg[p, row - 12 * p : end - 12 * p] = r3[which, d, row - 9 * d : end - 9 * d]
                row = end
        cells = dot(tys[...], jnp.concatenate([yg[p] for p in range(12)], axis=1), HIGH)
        for u in range(3):
            re = jnp.zeros((LY, 128), F32)
            im = jnp.zeros((LY, 128), F32)
            for k in range(4):
                at = 128 * (4 * u + k)
                cell = cells[:, at : at + 128]
                cosine = cell[0:8] + pltpu.roll(cell[8:16], 64, 1)
                sine = cell[16:24] + pltpu.roll(cell[24:32], 64, 1)
                both = cosine + jnp.where(
                    lane < 32, -pltpu.roll(sine, 96, 1), pltpu.roll(sine, 32, 1)
                )
                mine = lane // 32 == k
                up = 32 * k
                down = (32 * k + 96) % 128
                re = jnp.where(mine, pltpu.roll(both, up, 1) if up else both, re)
                im = jnp.where(mine, pltpu.roll(both, down, 1) if down else both, im)
            s4[which, u] = jnp.concatenate([re, im], axis=0).astype(BF16)
        start, arrived, done = exchange("gx", s4.at[which], r4.at[which], 2 + which, False, 3)
        start_all(start)
        r4[which, pl.ds(3 * gx, 3)] = s4[which]
        return arrived, done

    def cells_of(which):
        def step(jj, acc):
            acc = list(acc)
            for t in range(3):
                ix = 3 * jj + t
                for h in range(2):
                    unit = r4[which, 6 * jj + 2 * t + h].astype(F32)
                    re = unit[0:8]
                    im = unit[8:16]
                    for x in range(LX):
                        c = tx[gx, ix * 8 + 2 * x]
                        s = tx[gx, ix * 8 + 2 * x + 1]
                        at = (h * LX + x) * 2
                        acc[at] = acc[at] + (c * re - s * im)
                        acc[at + 1] = acc[at + 1] + (c * im + s * re)
            return tuple(acc)

        zero = jnp.zeros((LY, 128), F32)
        acc = lax.fori_loop(0, 8, step, (zero,) * 16)
        rows = [
            jnp.concatenate([acc[x * 2], acc[x * 2 + 1], acc[8 + x * 2], acc[9 + x * 2]], axis=1)
            for x in range(LX)
        ]
        modes = jnp.concatenate(rows, axis=0)
        high = modes.astype(BF16)
        low = (modes - high.astype(F32)).astype(BF16)
        return dot(high, mzs[0]) + (dot(high, mzs[1]) + dot(low, mzs[0]))

    def windows(dst, i, values):
        n = values.shape[0]
        zb = lax.broadcasted_iota(jnp.int32, (n, 8, 128), 1)
        ln = lax.broadcasted_iota(jnp.int32, (n, 8, 128), 2)
        before = pltpu.roll(values, 1, 1)
        after = pltpu.roll(values, 7, 1)
        edge = jnp.where(
            (ln >= 96) & (zb > 0), before, jnp.where((ln < 32) & (zb < 7), after, 0.0)
        )
        for part, lanes in ((values, 0), (edge, 128)):
            even = part.reshape(n // 2, 16, 128).astype(BF16)
            odd = part[1 : n - 1].reshape(n // 2 - 1, 16, 128).astype(BF16)
            dst[0, i, :, :, lanes : lanes + 128] = even
            dst[1, i, 0 : n // 2 - 1, :, lanes : lanes + 128] = odd

    def conv(src, kernel, nx, ny, acc):
        total = jnp.zeros((nx * ny * 8, 128), F32)
        for ab in range(9):
            a, b = divmod(ab, 3)
            rows = src[b % 2, a : a + nx, b // 2 : b // 2 + ny // 2].reshape(nx * ny * 8, 256)
            total = total + dot(rows, band[kernel, ab])
        acc[...] = total

    def correlate(src, off, grad, q):
        turned = grad.T.astype(BF16)

        lanes = lax.broadcasted_iota(jnp.int32, (C, 256), 1)
        for ab in range(9):
            a, b = divmod(ab, 3)
            a, b = a + off, b + off
            rows = src[b % 2, a : a + LX, b // 2 : b // 2 + LY // 2].reshape(256, 256)
            prod = dot(turned, rows)
            group, place = divmod(ab * 3, 4)
            first_lane = 32 * place
            acc = jnp.zeros((C, 256), F32)
            for zl in range(4):
                shift = (32 - 32 * zl + first_lane) % 256
                piece = prod[32 * zl : 32 * zl + 32]
                acc = acc + (pltpu.roll(piece, shift, 1) if shift else piece)
            acc = jnp.where((lanes >= first_lane) & (lanes < first_lane + 96), acc, 0.0)
            kgf[q, 32 * group : 32 * group + 32] += acc[:, 0:128]
            if first_lane + 96 > 128:
                kgf[q, 32 * group + 32 : 32 * group + 64] += acc[:, 128:256]
        for d in range(PEERS):
            kgb[q, d] = kgf[q, 14 * d : 14 * d + 16].astype(BF16)

    def grad_scatter(q):
        start, arrived, done = exchange("xy", kgb.at[q], r5.at[q], 4 + q, True, 1)
        start_all(start)
        r5[q, px * 4 + py] = kgb[q, px * 4 + py]
        return arrived, done

    def grad_sum(q):
        s6[q, 0] = total_of(r5.at[q], 1)[0, 0:14]
        start, arrived, done = exchange("z", s6.at[q], r6.at[q], 8 + q, False, 1)
        start_all(start)
        r6[q, zl * 4 + zc] = s6[q, 0]
        return arrived, done

    def grad_gather(q):
        s7[q] = total_of(r6.at[q], 1)
        start, arrived, done = exchange("xy", s7.at[q], r7.at[q], 6 + q, False, 1)
        start_all(start)
        r7[q, px * 4 + py] = s7[q, 0]
        return arrived, done

    def widen(ext, dst):
        @pl.loop(0, 8)
        def _(i):
            values = ext[i].astype(F32).reshape(12, 8, 128)
            yi = lax.broadcasted_iota(jnp.int32, (12, 8, 128), 0) + (gy * LY - 2)
            row = gx * LX - 2 + i
            ok = (row >= 0) & (row < NX) & (yi >= 0) & (yi < NY)
            windows(dst, i, jnp.where(ok, values, 0.0))

    for x in range(LX):
        mine = field[x].astype(F32)
        g = cot[x].astype(F32)
        for b in range(8):
            sp[8 * x : 8 * x + 8, b, :] = mine[:, 128 * b : 128 * b + 128]
            cg[8 * x : 8 * x + 8, b, :] = g[:, 128 * b : 128 * b + 128]
    xe[2:6, 1:5] = sp[...].reshape(4, 4, 16, 128).astype(BF16)
    spread(fz, mz, NZ, 2 * MZ * C)
    z_modes(field[...].reshape(32, 1024))

    pl.semaphore_wait(barrier, 2 * (PEERS - 1) + 22)

    x_arrived, x_done = x_send(0)

    for load in loads[:4]:
        load.wait()
    group = lax.broadcasted_iota(jnp.int32, (C, 128), 1) // C
    for q, kernel in ((0, k1), (1, k2)):

        @pl.loop(0, 9)
        def _(ab):
            wide = []
            for e in range(3):
                tap = kernel[3 * ab + e].astype(F32)
                wide.append(jnp.concatenate([tap] * 4, axis=1))
            for block in range(8):
                z = block if block < 5 else block - 8
                rows = jnp.zeros((C, 128), F32)
                for e in range(3):
                    if 0 <= z + 1 - e < 4:
                        rows = jnp.where(group == z + 1 - e, wide[e], rows)
                taps[32 * block : 32 * block + 32] = rows
            band[q, ab] = taps[...].astype(BF16)
            band[3 - q, 8 - ab, 0:128] = taps[0:128].T.astype(BF16)
            band[3 - q, 8 - ab, 128:256] = taps[128:256].T.astype(BF16)

    kgf[...] = jnp.zeros_like(kgf)
    yg[...] = jnp.zeros_like(yg)


    spread(fzs, mzs, 2 * MZ, NZ * C)
    wait_all(x_arrived)
    y_arrived, y_done = y_send(0)


    wait_all(y_arrived)
    loads[4].wait()
    first = (gx * PEERS + gy) * 18

    def scale_of(m):
        kz = lax.rem((first + m) // MY, MZ)
        return jnp.where(kz == 0, 1.0 / (NX * NY * NZ), 2.0 / (NX * NY * NZ)).astype(F32)

    xs[...] = jnp.zeros_like(xs)
    xs[0:9] = total_of(r2.at[0], 1)[0]
    xt[...] = xs[...].T
    for t in range(9):
        row = []
        for half in range(2):
            m = 2 * t + half
            xr = xt[64 * half : 64 * half + 32, t : t + 1]
            xi = xt[64 * half + 32 : 64 * half + 64, t : t + 1]
            wr = sw[0, m]
            wi = sw[1, m]
            row.append(jnp.sum(xr * wr - xi * wi, axis=0, keepdims=True) * scale_of(m))
            row.append(jnp.sum(xr * wi + xi * wr, axis=0, keepdims=True) * scale_of(m))
        s3[0, 0, t : t + 1, :] = jnp.concatenate(row, axis=1)
    m_arrived, m_done = modes_send(0)
    rim_send(xe, 0)


    wait_all(m_arrived)
    c_arrived, c_done = columns_send(0)
    rim_wait(xe, 0)
    widen(xe, xw)
    conv(xw, 0, 6, 10, pre)

    @pl.loop(0, 6)
    def _(i):
        rows = pl.ds(pl.multiple_of(i * 80, 80), 80)
        h, slope = gelu_parts(pre[rows])
        pre[rows] = slope
        yi = lax.broadcasted_iota(jnp.int32, (10, 8, 128), 0) + (gy * LY - 1)
        row = gx * LX - 1 + i
        ok = (row >= 0) & (row < NX) & (yi >= 0) & (yi < NY)
        h = h.astype(BF16).astype(F32).reshape(10, 8, 128)
        windows(hw, i, jnp.where(ok, h, 0.0))

    conv(hw, 1, 4, 8, brn)

    wait_all(c_arrived)
    spectral = cells_of(0)
    for b in range(8):
        sp[:, b, :] = spectral[:, 128 * b : 128 * b + 128]

    _, slope = gelu_parts(sp[...].reshape(256, 128) + brn[...])
    dtotal = (cg[...].reshape(256, 128) * slope).astype(BF16)
    de[2:6, 1:5] = dtotal.reshape(4, 4, 16, 128)
    rim_send(de, 1)
    dts[...] = dtotal.astype(F32).reshape(32, 8, 128)
    for b in range(8):
        dtl[:, 128 * b : 128 * b + 128] = dts[:, b, :].astype(BF16)
    z_modes(dtl[...])
    x_arrived2, x_done2 = x_send(1)

    correlate(hw, 0, dts[...].reshape(256, 128), 1)
    k_arrived2, k_done2 = grad_scatter(1)
    rim_wait(de, 1)
    widen(de, dw)
    conv(dw, 2, 6, 10, wide)

    @pl.loop(0, 6)
    def _(i):
        rows = pl.ds(pl.multiple_of(i * 80, 80), 80)
        dpre = (wide[rows] * pre[rows]).astype(BF16).astype(F32).reshape(10, 8, 128)
        yi = lax.broadcasted_iota(jnp.int32, (10, 8, 128), 0) + (gy * LY - 1)
        row = gx * LX - 1 + i
        ok = (row >= 0) & (row < NX) & (yi >= 0) & (yi < NY)
        windows(pw, i, jnp.where(ok, dpre, 0.0))

    own = pw[1, 1:5, 0:4, :, 0:128].reshape(256, 128).astype(F32)
    correlate(xw, 1, own, 0)
    k_arrived, k_done = grad_scatter(0)

    wait_all(x_arrived2)
    y_arrived2, y_done2 = y_send(1)
    wait_all(k_arrived2)
    l_arrived2, l_done2 = grad_sum(1)
    conv(pw, 3, 4, 8, brn)
    wait_all(k_arrived)
    l_arrived, l_done = grad_sum(0)

    wait_all(y_arrived2)
    xs[0:9] = total_of(r2.at[1], 1)[0]
    mode_lane = lax.broadcasted_iota(jnp.int32, (128, 128), 1)
    back = jnp.zeros((128, 128), F32)
    for t in range(9):
        column = []
        dy = xs[t : t + 1, :] * scale_of(2 * t)
        dys[t : t + 1, :] = dy
        for half in range(2):
            m = 2 * t + half
            wr = sw[0, m]
            wi = sw[1, m]
            dyr = dy[:, 64 * half : 64 * half + 32]
            dyi = dy[:, 64 * half + 32 : 64 * half + 64]
            column.append(jnp.sum(wr * dyr + wi * dyi, axis=1, keepdims=True))
            column.append(jnp.sum(wr * dyi - wi * dyr, axis=1, keepdims=True))
        back = jnp.where(mode_lane == t, jnp.concatenate(column, axis=0), back)
    xs[...] = back.T
    s3[1, 0] = xs[0:9]
    m_arrived2, m_done2 = modes_send(1)
    for t in range(9):
        for half in range(2):
            m = 2 * t + half
            xr = xt[64 * half : 64 * half + 32, t : t + 1]
            xi = xt[64 * half + 32 : 64 * half + 64, t : t + 1]
            dyr = dys[t : t + 1, 64 * half : 64 * half + 32]
            dyi = dys[t : t + 1, 64 * half + 32 : 64 * half + 64]
            sg[0, m] = xr * dyr + xi * dyi
            sg[1, m] = xr * dyi - xi * dyr
    save = pltpu.make_async_copy(sg, out_sg, ls.at[5])
    save.start()

    wait_all(m_arrived2)
    c_arrived2, c_done2 = columns_send(1)

    wait_all(l_arrived2)
    n_arrived2, n_done2 = grad_gather(1)
    wait_all(l_arrived)
    n_arrived, n_done = grad_gather(0)

    wait_all(c_arrived2)
    spectral = cells_of(1)
    dts[...] = brn[...].reshape(32, 8, 128)
    for b in range(8):
        value = spectral[:, 128 * b : 128 * b + 128] + dts[:, b, :]
        out_field[:, :, 128 * b : 128 * b + 128] = value.reshape(LX, LY, 128).astype(BF16)
    for q, waiting, out in ((1, n_arrived2, out_k2), (0, n_arrived, out_k1)):
        wait_all(waiting)
        for d in range(PEERS):
            kgf[q, 14 * d : 14 * d + 14] = r7[q, d]
        for group in range(7):
            turned = kgf[q, 32 * group : 32 * group + 32].T
            for place in range(min(4, 27 - 4 * group)):
                out[4 * group + place] = turned[32 * place : 32 * place + 32]

    save.wait()
    rim_done(xe, 0)
    rim_done(de, 1)
    for done in (
        x_done, y_done, m_done, c_done, x_done2, y_done2, m_done2, c_done2, k_done, l_done, n_done,
        k_done2, l_done2, n_done2,
    ):
        done()


def hand_over(*refs):
    results, outs, kept_here = refs[0:4], refs[4:8], refs[8:12]
    into, out = refs[12:14]
    loads = [pltpu.make_async_copy(results[i], kept_here[i], into.at[i]) for i in range(4)]
    saves = [pltpu.make_async_copy(kept_here[i], outs[i], out.at[i]) for i in range(4)]
    for load in loads:
        load.start()
    for load, save in zip(loads, saves):
        load.wait()
        save.start()
    for save in saves:
        save.wait()


def shards(field, cotangent, kernel_one, kernel_two, spectral_weight):
    mz, mzs, tx, ty, tys = constants()
    vmem = pl.BlockSpec(memory_space=pltpu.VMEM)
    hbm = pl.BlockSpec(memory_space=pl.ANY)
    smem = pl.BlockSpec(memory_space=pltpu.SMEM)

    def buf(shape, dtype=F32):
        return pltpu.VMEM(shape, dtype)

    results = pl.pallas_call(
        body,
        out_shape=(
            jax.ShapeDtypeStruct((LX, LY, NZ * C), BF16),
            jax.ShapeDtypeStruct((27, C, C), F32),
            jax.ShapeDtypeStruct((27, C, C), F32),
            jax.ShapeDtypeStruct(spectral_weight.shape, F32),
        ),
        in_specs=[vmem, vmem, hbm, hbm, hbm, vmem, vmem, smem, hbm, hbm],
        out_specs=(vmem, vmem, vmem, hbm),
        scratch_shapes=[
            buf((27, C, C), BF16),
            buf((27, C, C), BF16),
            buf((32, 16)),
            buf((32, 16)),
            buf(spectral_weight.shape),
            buf(spectral_weight.shape),
            buf((2, NZ * C, 2 * MZ * C), BF16),
            buf((2, 2 * MZ * C, NZ * C), BF16),
            buf((256, 128)),
            buf((480, 128)),
            buf((8, 6, 16, 128), BF16),
            buf((8, 6, 16, 128), BF16),
            buf((2, 8, 6, 16, 256), BF16),
            buf((2, 6, 5, 16, 256), BF16),
            buf((2, 8, 6, 16, 256), BF16),
            buf((2, 6, 5, 16, 256), BF16),
            buf((480, 128)),
            buf((256, 128)),
            buf((4, 9, 256, 128), BF16),
            buf((32, 8, 128)),
            buf((2, LX, LY, 256)),
            buf((32, 8, 128)),
            buf((32, 8, 128)),
            buf((32, 1024), BF16),
            buf((2, 48, 16, 128), BF16),
            buf((2, 48, 16, 128), BF16),
            buf((2, PEERS, 9, 128)),
            buf((2, PEERS, 9, 128)),
            buf((128, 128)),
            buf((128, 128)),
            buf((16, 128)),
            buf((144, 128)),
            buf((12, 16, 128)),
            buf((2, 1, 9, 128)),
            buf((2, PEERS, 9, 128)),
            buf((2, 3, 16, 128), BF16),
            buf((2, 48, 16, 128), BF16),
            buf((2, 256, 128)),
            buf((2, PEERS, 16, 128), BF16),
            buf((2, PEERS, 16, 128), BF16),
            buf((2, 1, 14, 128)),
            buf((2, PEERS, 14, 128)),
            buf((2, 1, 14, 128)),
            buf((2, PEERS, 14, 128)),
            pltpu.SemaphoreType.DMA((2, 8)),
            pltpu.SemaphoreType.DMA((2, 8)),
            pltpu.SemaphoreType.DMA((10, PEERS)),
            pltpu.SemaphoreType.DMA((10, PEERS)),
            pltpu.SemaphoreType.DMA((4, PEERS)),
            pltpu.SemaphoreType.DMA((4, PEERS)),
            pltpu.SemaphoreType.DMA((6,)),
        ],
        compiler_params=pltpu.CompilerParams(
            collective_id=0, has_side_effects=True, vmem_limit_bytes=56 << 20
        ),
    )(field, cotangent, kernel_one, kernel_two, spectral_weight, mz, mzs, tx, ty, tys)
    return pl.pallas_call(
        hand_over,
        out_shape=tuple(jax.ShapeDtypeStruct(r.shape, r.dtype) for r in results),
        in_specs=[hbm] * 4,
        out_specs=(hbm,) * 4,
        scratch_shapes=[buf(r.shape, r.dtype) for r in results]
        + [pltpu.SemaphoreType.DMA((4,)), pltpu.SemaphoreType.DMA((4,))],
    )(*results)


def solution(mesh):
    return jax.shard_map(
        shards,
        mesh=mesh,
        in_specs=(
            P("gx", "gy", None),
            P("gx", "gy", None),
            P(),
            P(),
            P(None, ("gx", "gy"), None, None),
        ),
        out_specs=(P("gx", "gy", None), P(), P(), P(None, ("gx", "gy"), None, None)),
        check_vma=False,
    )
```
